256 devices in a mesh: wide: 128 (over x, z, y), narrow: 2 (over core).
Axes of the slice: x: 4, y: 4, z: 8, core: 2. Of those that a mesh axis runs over, the one named last changes fastest.
Arguments:
- first_a: float32 [4096, 128], P(('wide', 'narrow')), may hold values from -42 to 42
- first_b: float32 [4096, 128], P(('wide', 'narrow')), may hold values from -42 to 42
- middle_a: float32 [128, 4096, 128], P(None, ('wide', 'narrow')), may hold values from -4.2 to 4.2
- middle_b: float32 [128, 4096, 128], P(None, ('wide', 'narrow')), may hold values from -4.2 to 4.2
- last_a: float32 [128, 4096, 128], P(None, ('wide', 'narrow')), may hold values from -0.5 to 0.5
- last_b: float32 [128, 4096, 128], P(None, ('wide', 'narrow')), may hold values from -0.5 to 0.5
Outputs:
- ortho_first: float32 [4096, 256], P(('wide', 'narrow'))
- ortho_middle: float32 [256, 4096, 256], P(None, ('wide', 'narrow'))
- next_core: float32 [256, 4096, 256], P(None, ('wide', 'narrow'))
The draws below stay inside these ranges and needn't reach their ends.
All inputs are finite; a program needn't handle non-finite values.
Results may differ from the reference program's by a relative error of at most 0.000086.
Values sent between devices are 32-bit elements; how exact they have to be, the bound alone decides.
A program may use at most 128 MiB of HBM per device.

```python
import jax
import jax.numpy as jnp
from jax import lax

RA = 128
N = 4096


def mode_scales(key, mode_count, salt_value):
    positions = jnp.arange(mode_count, dtype=jnp.float32) / max(mode_count - 1, 1)
    growth = 3.0
    jitter_factor = jnp.exp(jax.random.uniform(jax.random.fold_in(key, salt_value), (mode_count,), jnp.float32, -0.35, 0.35))
    return growth ** positions * jitter_factor


def core_entries(key, shape_full, salt_value):
    values = jnp.clip(jax.random.normal(jax.random.fold_in(key, salt_value), shape_full, jnp.float32), -5.0, 5.0)
    return values


def draw_first_a(key, part):
    return core_entries(key, (N, RA), 1) * mode_scales(key, N, 40)[:, None]


def draw_first_b(key, part):
    return core_entries(key, (N, RA), 2) * mode_scales(key, N, 40)[:, None]


def draw_middle_a(key, part):
    return 0.1 * core_entries(key, (RA, N, RA), 3) * mode_scales(key, N, 41)[None, :, None]


def draw_middle_b(key, part):
    return 0.1 * core_entries(key, (RA, N, RA), 4) * mode_scales(key, N, 41)[None, :, None]


def block_scale(own_key, extent, pieces, low, high):
    def one(position, parts):
        steps = jax.random.uniform(jax.random.fold_in(jax.random.fold_in(own_key, 6), position), (parts,), jnp.float32, low / len(pieces), high / len(pieces))
        return jnp.repeat(jnp.exp(steps), extent[position] // parts).reshape((-1,) + (1,) * (len(extent) - position - 1))

    factor_of = one(*pieces[0])
    for cut in pieces[1:]:
        factor_of = factor_of * one(*cut)
    return factor_of


def centred(key, shape, scale, most, pieces=(), held_as=jnp.bfloat16):
    array = scale * jax.random.normal(key, shape, jnp.float32)
    if pieces:
        array = array * block_scale(key, shape, pieces, -0.22, 0.18)
    return jnp.clip(array, -most, most).astype(held_as)


def setup_inputs(seed: int = 0) -> dict:
    keys = jax.random.split(jax.random.key(seed), 7)
    return {
        "first_a": draw_first_a(jax.random.fold_in(keys[6], 71), 0),
        "first_b": draw_first_b(jax.random.fold_in(keys[6], 71), 0),
        "middle_a": draw_middle_a(jax.random.fold_in(keys[6], 71), 0),
        "middle_b": draw_middle_b(jax.random.fold_in(keys[6], 71), 0),
        "last_a": centred(keys[4], (RA, N, RA), RA ** -0.5, 0.5, ((1, 256),), jnp.float32),
        "last_b": centred(keys[5], (RA, N, RA), RA ** -0.5, 0.5, ((1, 256),), jnp.float32),
    }


HIGHEST_PRECISION = lax.Precision.HIGHEST

def gram_matrix(matrix_rows):
    return lax.dot_general(matrix_rows.astype(jnp.float32), matrix_rows.astype(jnp.float32), (((0,), (0,)), ((), ())), precision=HIGHEST_PRECISION, preferred_element_type=jnp.float32)

def invert_factor(factor_low):
    identity = jnp.eye(factor_low.shape[0], dtype=jnp.float32)
    inverse_low = jax.scipy.linalg.solve_triangular(factor_low, identity, lower=True)
    return (factor_low.T, inverse_low.T)

def carry_factor(factor_up, block_first, block_second):
    half_rank = block_first.shape[0]
    mode_count = block_first.shape[1]
    flat_first = block_first.reshape(half_rank, -1)
    flat_second = block_second.reshape(half_rank, -1)
    top_first = jnp.dot(factor_up[:half_rank, :half_rank].astype(jnp.float32), flat_first.astype(jnp.float32), precision=HIGHEST_PRECISION, preferred_element_type=jnp.float32)
    top_second = jnp.dot(factor_up[:half_rank, half_rank:].astype(jnp.float32), flat_second.astype(jnp.float32), precision=HIGHEST_PRECISION, preferred_element_type=jnp.float32)
    low_second = jnp.dot(factor_up[half_rank:, half_rank:].astype(jnp.float32), flat_second.astype(jnp.float32), precision=HIGHEST_PRECISION, preferred_element_type=jnp.float32)
    shape_block = (half_rank, mode_count, half_rank)
    upper_rows = jnp.concatenate([top_first.reshape(shape_block), top_second.reshape(shape_block)], axis=2)
    lower_rows = jnp.concatenate([jnp.zeros(shape_block, jnp.float32), low_second.reshape(shape_block)], axis=2)
    return jnp.concatenate([upper_rows, lower_rows], axis=0)

def reference(first_a, first_b, middle_a, middle_b, last_a, last_b):
    first_rows = jnp.concatenate([first_a, first_b], axis=1)
    gram_one = gram_matrix(first_rows) / first_rows.shape[0]
    factor_one, inverse_one = invert_factor(jnp.linalg.cholesky(gram_one))
    ortho_first = jnp.dot(first_rows.astype(jnp.float32), inverse_one.astype(jnp.float32), precision=HIGHEST_PRECISION, preferred_element_type=jnp.float32)
    carried = carry_factor(factor_one, middle_a, middle_b)
    full_rank = carried.shape[2]
    middle_rows = carried.reshape(-1, full_rank)
    gram_two = gram_matrix(middle_rows) / middle_rows.shape[0]
    factor_two, inverse_two = invert_factor(jnp.linalg.cholesky(gram_two))
    ortho_middle = jnp.dot(middle_rows.astype(jnp.float32), inverse_two.astype(jnp.float32), precision=HIGHEST_PRECISION, preferred_element_type=jnp.float32).reshape(carried.shape)
    next_core = carry_factor(factor_two, last_a, last_b)
    return (ortho_first, ortho_middle, next_core)
```

```python
import functools

import jax
import jax.numpy as jnp
from jax import lax
from jax.experimental import pallas as pl
from jax.experimental.pallas import tpu as pltpu
from jax.sharding import PartitionSpec as P

MESH = pl.DeviceIdType.MESH
HIGHEST_PRECISION = lax.Precision.HIGHEST
PLANE = 32
DEPTH = 8
RANK = 128
FULL = 256
MODES = 16


def dot_f32(left, right, dims):
    return lax.dot_general(
        left, right, (dims, ((), ())), precision=HIGHEST_PRECISION, preferred_element_type=jnp.float32
    )


def gram_kernel(
    first_a, first_b, middle_a, middle_b, gram_one, gram_two,
    held_a, held_b, local_one, local_two, total_one, total_two, part_in, piece_out, piece_in,
    load_sem, send_sem, recv_sem,
):
    wide = lax.axis_index("wide")
    core = lax.axis_index("narrow")
    spot_x = wide // 32
    spot_z = (wide // 4) % 8
    spot_y = wide % 4
    mine = (spot_x * 4 + spot_y) * 2 + core

    def plane_device(step):
        peer = (mine + step) % PLANE
        return peer, ((peer // 8) * 32 + spot_z * 4 + (peer // 2) % 4, peer % 2)

    def line_device(step):
        return (spot_x * 32 + ((spot_z + step) % DEPTH) * 4 + spot_y, core)

    barrier = pltpu.get_barrier_semaphore()

    def greet_plane(step, carry):
        pl.semaphore_signal(barrier, inc=1, device_id=plane_device(step)[1], device_id_type=MESH)
        return carry

    def greet_line(step, carry):
        pl.semaphore_signal(barrier, inc=1, device_id=line_device(step), device_id_type=MESH)
        return carry

    lax.fori_loop(1, PLANE, greet_plane, 0)
    lax.fori_loop(1, DEPTH, greet_line, 0)

    loads = []
    for mode in range(MODES):
        for side, (source, target) in enumerate(((middle_a, held_a), (middle_b, held_b))):
            load = pltpu.make_async_copy(source.at[:, mode, :], target.at[mode], load_sem.at[side, mode])
            load.start()
            loads.append(load)

    rows = jnp.concatenate([first_a[...], first_b[...]], axis=1)
    local_one[...] = dot_f32(rows, rows, ((0,), (0,))).reshape(PLANE, 8, FULL)
    pl.semaphore_wait(barrier, PLANE - 1 + DEPTH - 1)

    def reduce_all(turn, local, total, scale):
        def scatter(step, carry):
            peer, device = plane_device(step)
            pltpu.make_async_remote_copy(
                src_ref=local.at[peer],
                dst_ref=part_in.at[turn, step - 1],
                send_sem=send_sem.at[turn, 0],
                recv_sem=recv_sem.at[turn, 0],
                device_id=device,
                device_id_type=MESH,
            ).start()
            return carry

        lax.fori_loop(1, PLANE, scatter, 0)

        def wait_plane(phase, buffer):
            copy = pltpu.make_async_remote_copy(
                src_ref=buffer,
                dst_ref=buffer,
                send_sem=send_sem.at[turn, phase],
                recv_sem=recv_sem.at[turn, phase],
                device_id=(wide, core),
                device_id_type=MESH,
            )
            copy.wait_recv()
            copy.wait_send()

        wait_plane(0, part_in.at[turn])
        piece_out[turn] = local[mine] + jnp.sum(part_in[turn], axis=0)

        def line(step, carry):
            pltpu.make_async_remote_copy(
                src_ref=piece_out.at[turn],
                dst_ref=piece_in.at[turn, step - 1],
                send_sem=send_sem.at[turn, 1],
                recv_sem=recv_sem.at[turn, 1],
                device_id=line_device(step),
                device_id_type=MESH,
            ).start()
            return carry

        lax.fori_loop(1, DEPTH, line, 0)
        wait_plane(1, piece_in.at[turn])
        total[mine] = (piece_out[turn] + jnp.sum(piece_in[turn], axis=0)) * scale

        def gather(step, carry):
            peer, device = plane_device(step)
            pltpu.make_async_remote_copy(
                src_ref=total.at[mine],
                dst_ref=total.at[mine],
                send_sem=send_sem.at[turn, 2],
                recv_sem=recv_sem.at[turn, 2],
                device_id=device,
                device_id_type=MESH,
            ).start()
            return carry

        lax.fori_loop(1, PLANE, gather, 0)
        wait_plane(2, total.at[pl.ds(0, PLANE - 1)])

    reduce_all(0, local_one, total_one, 1.0 / 4096)
    gram = total_one[...].reshape(FULL, FULL)
    gram_one[...] = gram
    for load in loads:
        load.wait()
    gram_aa = gram[:RANK, :RANK]
    gram_ab = gram[:RANK, RANK:]
    gram_bb = gram[RANK:, RANK:]

    def carry_mode(mode, sums):
        sum_aa, sum_ab, sum_bb = sums
        block_a = held_a[mode]
        block_b = held_b[mode]
        over = ((1,), (0,))
        rows = ((0,), (0,))
        sum_aa += dot_f32(block_a, dot_f32(gram_aa, block_a, over), rows)
        sum_ab += dot_f32(block_a, dot_f32(gram_ab, block_b, over), rows)
        sum_bb += dot_f32(block_b, dot_f32(gram_bb, block_b, over), rows)
        return sum_aa, sum_ab, sum_bb

    zero = jnp.zeros((RANK, RANK), jnp.float32)
    sum_aa, sum_ab, sum_bb = lax.fori_loop(0, MODES, carry_mode, (zero, zero, zero))
    local = jnp.concatenate(
        [jnp.concatenate([sum_aa, sum_ab], axis=1), jnp.concatenate([sum_ab.T, sum_bb], axis=1)], axis=0
    )
    local_two[...] = local.reshape(PLANE, 8, FULL)
    reduce_all(1, local_two, total_two, 1.0 / 1048576)
    gram_two[...] = total_two[...].reshape(FULL, FULL)


def both_grams(first_a, first_b, middle_a, middle_b):
    square = jax.ShapeDtypeStruct((FULL, FULL), jnp.float32)
    vmem = pl.BlockSpec(memory_space=pltpu.VMEM)
    whole = pl.BlockSpec(memory_space=pl.ANY)
    return pl.pallas_call(
        gram_kernel,
        out_shape=(square, square),
        in_specs=[vmem, vmem, whole, whole],
        out_specs=(vmem, vmem),
        scratch_shapes=[
            pltpu.VMEM((MODES, RANK, RANK), jnp.float32),
            pltpu.VMEM((MODES, RANK, RANK), jnp.float32),
            pltpu.VMEM((PLANE, 8, FULL), jnp.float32),
            pltpu.VMEM((PLANE, 8, FULL), jnp.float32),
            pltpu.VMEM((PLANE, 8, FULL), jnp.float32),
            pltpu.VMEM((PLANE, 8, FULL), jnp.float32),
            pltpu.VMEM((2, PLANE - 1, 8, FULL), jnp.float32),
            pltpu.VMEM((2, 8, FULL), jnp.float32),
            pltpu.VMEM((2, DEPTH - 1, 8, FULL), jnp.float32),
            pltpu.SemaphoreType.DMA((2, MODES)),
            pltpu.SemaphoreType.DMA((2, 3)),
            pltpu.SemaphoreType.DMA((2, 3)),
        ],
        compiler_params=pltpu.CompilerParams(
            collective_id=0, has_side_effects=True, vmem_limit_bytes=32 * 1024 * 1024
        ),
    )(first_a, first_b, middle_a, middle_b)


def matmul_exact(matrix_left, matrix_right):
    return jnp.dot(
        matrix_left, matrix_right, precision=HIGHEST_PRECISION, preferred_element_type=jnp.float32
    )


def invert_factor(factor_low):
    identity = jnp.eye(factor_low.shape[0], dtype=jnp.float32)
    inverse_low = jax.scipy.linalg.solve_triangular(factor_low, identity, lower=True)
    return (factor_low.T, inverse_low.T)


def carry_factor(factor_up, block_first, block_second):
    half_rank = block_first.shape[0]
    mode_count = block_first.shape[1]
    shape_block = (half_rank, mode_count, half_rank)
    flat_first = block_first.reshape(half_rank, -1)
    flat_second = block_second.reshape(half_rank, -1)
    top_first = matmul_exact(factor_up[:half_rank, :half_rank], flat_first)
    top_second = matmul_exact(factor_up[:half_rank, half_rank:], flat_second)
    low_second = matmul_exact(factor_up[half_rank:, half_rank:], flat_second)
    upper_rows = jnp.concatenate(
        [top_first.reshape(shape_block), top_second.reshape(shape_block)], axis=2
    )
    lower_rows = jnp.concatenate(
        [jnp.zeros(shape_block, jnp.float32), low_second.reshape(shape_block)], axis=2
    )
    return jnp.concatenate([upper_rows, lower_rows], axis=0)


def body(first_a, first_b, middle_a, middle_b, last_a, last_b):
    gram_one, gram_two = both_grams(first_a, first_b, middle_a, middle_b)
    first_rows = jnp.concatenate([first_a, first_b], axis=1)
    factor_one, inverse_one = invert_factor(jnp.linalg.cholesky(gram_one))
    ortho_first = matmul_exact(first_rows, inverse_one)
    carried = carry_factor(factor_one, middle_a, middle_b)
    middle_rows = carried.reshape(-1, FULL)
    factor_two, inverse_two = invert_factor(jnp.linalg.cholesky(gram_two))
    ortho_rows = matmul_exact(middle_rows, inverse_two)
    ortho_middle = ortho_rows.reshape(carried.shape)
    next_core = carry_factor(factor_two, last_a, last_b)
    return (ortho_first, ortho_middle, next_core)


def solution(mesh):
    placed = (
        P(("wide", "narrow"), None),
        P(("wide", "narrow"), None),
        P(None, ("wide", "narrow"), None),
        P(None, ("wide", "narrow"), None),
        P(None, ("wide", "narrow"), None),
        P(None, ("wide", "narrow"), None),
    )
    return jax.shard_map(
        body,
        mesh=mesh,
        in_specs=placed,
        out_specs=(
            P(("wide", "narrow"), None),
            P(None, ("wide", "narrow"), None),
            P(None, ("wide", "narrow"), None),
        ),
        check_vma=False,
    )
```

```python
import functools

import jax
import jax.numpy as jnp
from jax import lax
from jax.experimental import pallas as pl
from jax.experimental.pallas import tpu as pltpu
from jax.sharding import PartitionSpec as P

MESH = pl.DeviceIdType.MESH
HIGHEST_PRECISION = lax.Precision.HIGHEST
PLANE = 32
DEPTH = 8
RANK = 128
FULL = 256
MODES = 16
VMEM_BYTES = 60 * 1024 * 1024


def dot_f32(left, right, dims):
    return lax.dot_general(
        left, right, (dims, ((), ())), precision=HIGHEST_PRECISION, preferred_element_type=jnp.float32
    )


def gram_kernel(
    first_a, first_b, middle_a, middle_b, gram_one, gram_two,
    first_rows, held_a, held_b, local_one, local_two, total_one, total_two, part_in, piece_out, piece_in,
    first_sem, load_sem, send_sem, recv_sem,
):
    wide = lax.axis_index("wide")
    core = lax.axis_index("narrow")
    spot_x = wide // 32
    spot_z = (wide // 4) % 8
    spot_y = wide % 4
    mine = (spot_x * 4 + spot_y) * 2 + core

    def plane_device(step):
        peer = (mine + step) % PLANE
        return peer, ((peer // 8) * 32 + spot_z * 4 + (peer // 2) % 4, peer % 2)

    def line_device(step):
        return (spot_x * 32 + ((spot_z + step) % DEPTH) * 4 + spot_y, core)

    first_loads = []
    for side, source in enumerate((first_a, first_b)):
        load = pltpu.make_async_copy(source, first_rows.at[side], first_sem.at[side])
        load.start()
        first_loads.append(load)

    barrier = pltpu.get_barrier_semaphore()

    def greet_plane(step, carry):
        pl.semaphore_signal(barrier, inc=1, device_id=plane_device(step)[1], device_id_type=MESH)
        return carry

    def greet_line(step, carry):
        pl.semaphore_signal(barrier, inc=1, device_id=line_device(step), device_id_type=MESH)
        return carry

    lax.fori_loop(1, PLANE, greet_plane, 0)
    lax.fori_loop(1, DEPTH, greet_line, 0)

    loads = []
    for mode in range(MODES):
        for side, (source, target) in enumerate(((middle_a, held_a), (middle_b, held_b))):
            load = pltpu.make_async_copy(source.at[:, mode, :], target.at[mode], load_sem.at[side, mode])
            load.start()
            loads.append(load)

    for load in first_loads:
        load.wait()
    rows = jnp.concatenate([first_rows[0], first_rows[1]], axis=1)
    local_one[...] = dot_f32(rows, rows, ((0,), (0,))).reshape(PLANE, 8, FULL)
    pl.semaphore_wait(barrier, PLANE - 1 + DEPTH - 1)

    def reduce_all(turn, local, total, scale):
        def scatter(step, carry):
            peer, device = plane_device(step)
            pltpu.make_async_remote_copy(
                src_ref=local.at[peer],
                dst_ref=part_in.at[turn, step - 1],
                send_sem=send_sem.at[turn, 0],
                recv_sem=recv_sem.at[turn, 0],
                device_id=device,
                device_id_type=MESH,
            ).start()
            return carry

        lax.fori_loop(1, PLANE, scatter, 0)

        def wait_plane(phase, buffer):
            copy = pltpu.make_async_remote_copy(
                src_ref=buffer,
                dst_ref=buffer,
                send_sem=send_sem.at[turn, phase],
                recv_sem=recv_sem.at[turn, phase],
                device_id=(wide, core),
                device_id_type=MESH,
            )
            copy.wait_recv()
            copy.wait_send()

        wait_plane(0, part_in.at[turn])
        piece_out[turn] = local[mine] + jnp.sum(part_in[turn], axis=0)

        def line(step, carry):
            pltpu.make_async_remote_copy(
                src_ref=piece_out.at[turn],
                dst_ref=piece_in.at[turn, step - 1],
                send_sem=send_sem.at[turn, 1],
                recv_sem=recv_sem.at[turn, 1],
                device_id=line_device(step),
                device_id_type=MESH,
            ).start()
            return carry

        lax.fori_loop(1, DEPTH, line, 0)
        wait_plane(1, piece_in.at[turn])
        total[mine] = (piece_out[turn] + jnp.sum(piece_in[turn], axis=0)) * scale

        def gather(step, carry):
            peer, device = plane_device(step)
            pltpu.make_async_remote_copy(
                src_ref=total.at[mine],
                dst_ref=total.at[mine],
                send_sem=send_sem.at[turn, 2],
                recv_sem=recv_sem.at[turn, 2],
                device_id=device,
                device_id_type=MESH,
            ).start()
            return carry

        lax.fori_loop(1, PLANE, gather, 0)
        wait_plane(2, total.at[pl.ds(0, PLANE - 1)])

    reduce_all(0, local_one, total_one, 1.0 / 4096)
    gram = total_one[...].reshape(FULL, FULL)
    gram_one[...] = gram
    for load in loads:
        load.wait()
    gram_aa = gram[:RANK, :RANK]
    gram_ab = gram[:RANK, RANK:]
    gram_bb = gram[RANK:, RANK:]

    def carry_mode(mode, sums):
        sum_aa, sum_ab, sum_bb = sums
        block_a = held_a[mode]
        block_b = held_b[mode]
        over = ((1,), (0,))
        rows = ((0,), (0,))
        sum_aa += dot_f32(block_a, dot_f32(gram_aa, block_a, over), rows)
        sum_ab += dot_f32(block_a, dot_f32(gram_ab, block_b, over), rows)
        sum_bb += dot_f32(block_b, dot_f32(gram_bb, block_b, over), rows)
        return sum_aa, sum_ab, sum_bb

    zero = jnp.zeros((RANK, RANK), jnp.float32)
    sum_aa, sum_ab, sum_bb = lax.fori_loop(0, MODES, carry_mode, (zero, zero, zero))
    local = jnp.concatenate(
        [jnp.concatenate([sum_aa, sum_ab], axis=1), jnp.concatenate([sum_ab.T, sum_bb], axis=1)], axis=0
    )
    local_two[...] = local.reshape(PLANE, 8, FULL)
    reduce_all(1, local_two, total_two, 1.0 / 1048576)
    gram_two[...] = total_two[...].reshape(FULL, FULL)


def both_grams(first_a, first_b, middle_a, middle_b):
    square = jax.ShapeDtypeStruct((FULL, FULL), jnp.float32)
    vmem = pl.BlockSpec(memory_space=pltpu.VMEM)
    whole = pl.BlockSpec(memory_space=pl.ANY)
    return pl.pallas_call(
        gram_kernel,
        out_shape=(square, square),
        in_specs=[whole] * 4,
        out_specs=(vmem, vmem),
        scratch_shapes=[
            pltpu.VMEM((2, MODES, RANK), jnp.float32),
            pltpu.VMEM((MODES, RANK, RANK), jnp.float32),
            pltpu.VMEM((MODES, RANK, RANK), jnp.float32),
            pltpu.VMEM((PLANE, 8, FULL), jnp.float32),
            pltpu.VMEM((PLANE, 8, FULL), jnp.float32),
            pltpu.VMEM((PLANE, 8, FULL), jnp.float32),
            pltpu.VMEM((PLANE, 8, FULL), jnp.float32),
            pltpu.VMEM((2, PLANE - 1, 8, FULL), jnp.float32),
            pltpu.VMEM((2, 8, FULL), jnp.float32),
            pltpu.VMEM((2, DEPTH - 1, 8, FULL), jnp.float32),
            pltpu.SemaphoreType.DMA((2,)),
            pltpu.SemaphoreType.DMA((2, MODES)),
            pltpu.SemaphoreType.DMA((2, 3)),
            pltpu.SemaphoreType.DMA((2, 3)),
        ],
        compiler_params=pltpu.CompilerParams(
            collective_id=0, has_side_effects=True, vmem_limit_bytes=VMEM_BYTES
        ),
    )(first_a, first_b, middle_a, middle_b)


def spread_row(tile, row):
    return jnp.broadcast_to(tile[row : row + 1, :], (8, 128))


def spread_lane(tile, lane):
    return jnp.broadcast_to(tile[:, lane : lane + 1], (8, 128))


def eliminate_panel(matrices, uppers, start, stop, lanes, rows):
    for base in range(start, stop, 8):
        half, lane = base // 128, base % 128
        here = base // 8
        groups = list(range(here, stop // 8))
        inside = (lanes >= lane) & (lanes < lane + 8)
        columns = []
        for matrix in matrices:
            columns.append({g: [spread_lane(matrix[g][half], lane + t) for t in range(8)] for g in groups})
            for g in groups:
                unit = jnp.where(lanes == rows + lane, 1.0, 0.0) if g == here else 0.0
                matrix[g][half] = jnp.where(inside, unit, matrix[g][half])
        for t in range(8):
            live = groups if t < 7 else groups[1:]
            for matrix, column in zip(matrices, columns):
                inverse = 1.0 / spread_row(column[here][t], t)
                factors = {g: column[g][t] * inverse for g in live}
                if t < 7:
                    factors[here] = jnp.where(rows > t, factors[here], 0.0)
                for later in range(t + 1, 8):
                    entry = spread_row(column[here][later], t)
                    for g in live:
                        column[g][later] = column[g][later] - factors[g] * entry
                for side in (0, 1):
                    pivot_row = spread_row(matrix[here][side], t)
                    for g in live:
                        matrix[g][side] = matrix[g][side] - factors[g] * pivot_row
        for matrix, upper, column in zip(matrices, uppers, columns):
            pivots = column[here][0]
            top = matrix[here][half]
            for t in range(8):
                pivots = jnp.where(rows == t, column[here][t], pivots)
                top = jnp.where(lanes == lane + t, column[here][t], top)
            root = lax.rsqrt(pivots)
            top = top * root
            matrix[here] = [matrix[here][0] * root, matrix[here][1] * root]
            upper[here] = [top, matrix[here][1]] if half == 0 else [matrix[here][0], top]


def factor_squares(squares):
    panel = 64
    lanes = lax.broadcasted_iota(jnp.int32, (8, 128), 1)
    rows = lax.broadcasted_iota(jnp.int32, (8, 128), 0)
    matrices = [
        {g: [square[8 * g : 8 * g + 8, :128], square[8 * g : 8 * g + 8, 128:]] for g in range(32)}
        for square in squares
    ]
    uppers = [{} for _ in squares]
    for start in range(0, FULL, panel):
        stop = start + panel
        eliminate_panel(matrices, uppers, start, stop, lanes, rows)
        if stop == FULL:
            break
        row_index = lax.broadcasted_iota(jnp.int32, (panel, FULL), 0) + start
        lane_index = lax.broadcasted_iota(jnp.int32, (panel, FULL), 1)
        low = stop // 128 * 128
        for matrix in matrices:
            done = jnp.concatenate(
                [jnp.concatenate(matrix[g], axis=1) for g in range(start // 8, stop // 8)], axis=0
            )
            right = jnp.where((lane_index > row_index) & (lane_index < stop), 0.0, done)
            update = dot_f32(done[:, low:], right, ((0,), (0,)))
            for g in range(stop // 8, 32):
                for side in (0, 1):
                    first, last = start - side * 128, stop - side * 128
                    kept = matrix[g][side]
                    if 0 <= first < 128:
                        kept = jnp.where((lanes >= first) & (lanes < last), 0.0, kept)
                    matrix[g][side] = kept - update[8 * g - low : 8 * g - low + 8, side * 128 : side * 128 + 128]
    results = []
    for matrix, upper in zip(matrices, uppers):
        factor, inverse = [], []
        for g in range(32):
            row = rows + 8 * g
            factor.append(
                jnp.concatenate([jnp.where(lanes + 128 * s >= row, upper[g][s], 0.0) for s in (0, 1)], axis=1)
            )
            inverse.append(
                jnp.concatenate([jnp.where(lanes + 128 * s <= row, matrix[g][s], 0.0) for s in (0, 1)], axis=1)
            )
        results.append((jnp.concatenate(factor, axis=0), jnp.concatenate(inverse, axis=0)))
    return results


def split(value):
    high = value.astype(jnp.bfloat16)
    return high, (value - high.astype(jnp.float32)).astype(jnp.bfloat16)


def dot_split(left, right):
    def dot(one, other):
        return jnp.dot(one, other, preferred_element_type=jnp.float32)

    return dot(left[0], right[0]) + (dot(left[1], right[0]) + dot(left[0], right[1]))


def finish_kernel(
    gram_one, gram_two, first_a, first_b, middle_a, middle_b, last_a, last_b,
    ortho_first, ortho_middle, next_core,
    first, held, carried, following, load_sem, store_sem,
):
    loads = []
    for index, source in enumerate((middle_a, middle_b, last_a, last_b, first_a, first_b)):
        target = held.at[index] if index < 4 else first.at[index - 4]
        load = pltpu.make_async_copy(source, target, load_sem.at[index])
        load.start()
        loads.append(load)
    lower = pl.ds(RANK * MODES, RANK * MODES)
    carried[0, lower] = jnp.zeros((RANK * MODES, RANK), jnp.float32)
    following[0, lower] = jnp.zeros((RANK * MODES, RANK), jnp.float32)

    (factor_one, inverse_one), (factor_two, inverse_two) = factor_squares([gram_one[...], gram_two[...]])
    for load in loads:
        load.wait()
    first_rows = jnp.concatenate([first[0], first[1]], axis=1)
    ortho_first[...] = dot_f32(first_rows, inverse_one, ((1,), (1,)))

    def carry(factor, side, target):
        corner = split(factor[:RANK, :RANK])
        column = split(factor[:, RANK:])
        for mode in range(MODES):
            block_a = split(held[side, pl.ds(mode, RANK, stride=MODES), :])
            block_b = split(held[side + 1, pl.ds(mode, RANK, stride=MODES), :])
            target[0, pl.ds(mode, RANK, stride=MODES)] = dot_split(corner, block_a)
            target[1, pl.ds(mode, FULL, stride=MODES)] = dot_split(column, block_b)

    stores = []

    def send(buffer, target, part):
        for side in (0, 1):
            store = pltpu.make_async_copy(
                buffer.at[side, part], target.at[part, pl.ds(side * RANK, RANK)], store_sem.at[len(stores)]
            )
            store.start()
            stores.append(store)

    carry(factor_two, 2, following)
    send(following, next_core, pl.ds(0, FULL * MODES))
    carry(factor_one, 0, carried)
    inverse = inverse_two.T
    whole = split(inverse)
    corner = split(inverse[RANK:, RANK:])
    step = 512
    for start in range(0, RANK * MODES, step):
        part = pl.ds(start, step)
        result = dot_split(split(jnp.concatenate([carried[0, part], carried[1, part]], axis=1)), whole)
        carried[0, part] = result[:, :RANK]
        carried[1, part] = result[:, RANK:]
        send(carried, ortho_middle, part)
    for start in range(RANK * MODES, FULL * MODES, step):
        part = pl.ds(start, step)
        carried[1, part] = dot_split(split(carried[1, part]), corner)
        send(carried, ortho_middle, part)
    for store in stores:
        store.wait()


def finish(gram_one, gram_two, first_a, first_b, *blocks):
    vmem = pl.BlockSpec(memory_space=pltpu.VMEM)
    whole = pl.BlockSpec(memory_space=pl.ANY)
    rows = FULL * MODES
    flat = [block.reshape(RANK * MODES, RANK) for block in blocks]
    ortho_first, ortho_middle, next_core = pl.pallas_call(
        finish_kernel,
        out_shape=(
            jax.ShapeDtypeStruct((MODES, FULL), jnp.float32),
            jax.ShapeDtypeStruct((rows, FULL), jnp.float32),
            jax.ShapeDtypeStruct((rows, FULL), jnp.float32),
        ),
        in_specs=[vmem] * 2 + [whole] * 6,
        out_specs=(vmem, whole, whole),
        scratch_shapes=[
            pltpu.VMEM((2, MODES, RANK), jnp.float32),
            pltpu.VMEM((4, RANK * MODES, RANK), jnp.float32),
            pltpu.VMEM((2, rows, RANK), jnp.float32),
            pltpu.VMEM((2, rows, RANK), jnp.float32),
            pltpu.SemaphoreType.DMA((6,)),
            pltpu.SemaphoreType.DMA((18,)),
        ],
        compiler_params=pltpu.CompilerParams(vmem_limit_bytes=VMEM_BYTES),
    )(gram_one, gram_two, first_a, first_b, *flat)
    shape = (FULL, MODES, FULL)
    return ortho_first, ortho_middle.reshape(shape), next_core.reshape(shape)


def body(first_a, first_b, middle_a, middle_b, last_a, last_b):
    gram_one, gram_two = both_grams(first_a, first_b, middle_a, middle_b)
    return finish(gram_one, gram_two, first_a, first_b, middle_a, middle_b, last_a, last_b)


def solution(mesh):
    placed = (
        P(("wide", "narrow"), None),
        P(("wide", "narrow"), None),
        P(None, ("wide", "narrow"), None),
        P(None, ("wide", "narrow"), None),
        P(None, ("wide", "narrow"), None),
        P(None, ("wide", "narrow"), None),
    )
    return jax.shard_map(
        body,
        mesh=mesh,
        in_specs=placed,
        out_specs=(
            P(("wide", "narrow"), None),
            P(None, ("wide", "narrow"), None),
            P(None, ("wide", "narrow"), None),
        ),
        check_vma=False,
    )
```

```python
import jax
import jax.numpy as jnp
from jax import lax
from jax.experimental import pallas as pl
from jax.experimental.pallas import tpu as pltpu
from jax.sharding import PartitionSpec as P

MESH = pl.DeviceIdType.MESH
HIGHEST_PRECISION = lax.Precision.HIGHEST
PIECES = 32
CHIPS = 16
SIDE = 4
DEPTH = 8
RANK = 128
FULL = 256
MODES = 16
VMEM_BYTES = 60 * 1024 * 1024


def dot_f32(left, right, dims):
    return lax.dot_general(
        left, right, (dims, ((), ())), precision=HIGHEST_PRECISION, preferred_element_type=jnp.float32
    )


def far_first(offsets, sizes):
    def hops(offset):
        return sum(min(step, size - step) for step, size in zip(offset, sizes))

    return sorted((offset for offset in offsets if any(offset)), key=lambda offset: -hops(offset))


PLANE_STEPS = far_first([(x, y) for x in range(SIDE) for y in range(SIDE)], (SIDE, SIDE))
LINE_STEPS = far_first([(z,) for z in range(DEPTH)], (DEPTH,))


def split(value):
    high = value.astype(jnp.bfloat16)
    return high, (value - high.astype(jnp.float32)).astype(jnp.bfloat16)


def dot_half(left, right):
    return jnp.dot(left, right, preferred_element_type=jnp.float32)


def factor_steps(square, widths, refs=None):
    rest = square
    start = 0
    uppers, lowers = [], []
    for panel_rows in widths:
        stop = start + panel_rows
        if refs is not None and start:
            rest = refs[2][pl.ds(start, FULL - start), :]
        halves = [rest[:panel_rows, :128], rest[:panel_rows, 128:]]
        below = rest[panel_rows:]
        done = []
        for base in range(start, stop, 8):
            side, lane = base // 128, base % 128
            height = stop - base
            lanes = lax.broadcasted_iota(jnp.int32, (height, 128), 1)
            rows = lax.broadcasted_iota(jnp.int32, (height, 128), 0)
            columns = [
                jnp.broadcast_to(halves[side][:, lane + t : lane + t + 1], (height, 128)) for t in range(8)
            ]
            inside = (lanes >= lane) & (lanes < lane + 8)
            halves[side] = jnp.where(inside, jnp.where(lanes == rows + lane, 1.0, 0.0), halves[side])
            for t in range(8):
                inverse = 1.0 / columns[t][t : t + 1]
                column = jnp.where(rows > t, columns[t], 0.0)
                factors = column * inverse
                for later in range(t + 1, 8):
                    entry = columns[later][t : t + 1]
                    taken = (column * entry) * inverse if later == t + 1 else factors * entry
                    columns[later] = columns[later] - taken
                halves = [half - factors * half[t : t + 1] for half in halves]
            small, small_lanes = rows[:8], lanes[:8]
            pivots, top = columns[0][:8], halves[side][:8]
            for t in range(8):
                pivots = jnp.where(small == t, columns[t][:8], pivots)
                top = jnp.where(small_lanes == lane + t, columns[t][:8], top)
            root = lax.rsqrt(pivots)
            ready = [half[:8] * root for half in halves]
            done.append(jnp.concatenate(ready, axis=1))
            top = top * root
            upper = [top, ready[1]] if side == 0 else [ready[0], top]
            row = small + base
            uppers.append(
                jnp.concatenate([jnp.where(small_lanes + 128 * s >= row, upper[s], 0.0) for s in (0, 1)], axis=1)
            )
            lowers.append(
                jnp.concatenate([jnp.where(small_lanes + 128 * s <= row, ready[s], 0.0) for s in (0, 1)], axis=1)
            )
            halves = [half[8:] for half in halves]
            if base + 8 == stop and stop < FULL:
                done = jnp.concatenate(done, axis=0)
                row_index = lax.broadcasted_iota(jnp.int32, (panel_rows, FULL), 0) + start
                lane_index = lax.broadcasted_iota(jnp.int32, (panel_rows, FULL), 1)
                right = jnp.where((lane_index > row_index) & (lane_index < stop), 0.0, done)
                low = stop // 128 * 128
                update = dot_f32(done[:, low:], right, ((0,), (0,)))[stop - low :]
                below_lanes = lax.broadcasted_iota(jnp.int32, below.shape, 1)
                rest = jnp.where((below_lanes >= start) & (below_lanes < stop), 0.0, below) - update
                if refs is not None:
                    refs[2][pl.ds(stop, FULL - stop), :] = rest
            if refs is not None:
                refs[0][pl.ds(base, 8), :] = uppers.pop()
                refs[1][pl.ds(base, 8), :] = lowers.pop()
            yield
        start = stop
    yield jnp.concatenate(uppers, axis=0), jnp.concatenate(lowers, axis=0)


def gram_kernel(
    first_a, first_b, middle_a, middle_b, gram_two, factor_one, inverse_one,
    first_rows, held, local_one, local_two, total_one, total_two,
    half_in, half_out, part_in, piece_out, piece_in, pairs, pairs_turned, carried_top, carried_low, rest,
    load_sem, send_sem, recv_sem,
):
    wide = lax.axis_index("wide")
    core = lax.axis_index("narrow")
    spot_x = wide // 32
    spot_z = (wide // 4) % 8
    spot_y = wide % 4
    mine = core * CHIPS + spot_x * SIDE + spot_y
    base = core * CHIPS
    other = (wide, 1 - core)

    def plane_peer(step):
        x, y = (spot_x + step[0]) % SIDE, (spot_y + step[1]) % SIDE
        return base + x * SIDE + y, (x * 32 + spot_z * 4 + y, core)

    def line_device(step):
        return (spot_x * 32 + ((spot_z + step[0]) % DEPTH) * 4 + spot_y, core)

    loads = []
    for index, (source, target) in enumerate(
        ((first_a, first_rows.at[0]), (first_b, first_rows.at[1]), (middle_a, held.at[0]), (middle_b, held.at[1]))
    ):
        load = pltpu.make_async_copy(source, target, load_sem.at[index])
        load.start()
        loads.append(load)

    barrier = pltpu.get_barrier_semaphore()
    for step in LINE_STEPS:
        pl.semaphore_signal(barrier, inc=1, device_id=line_device(step), device_id_type=MESH)
    for step in PLANE_STEPS:
        pl.semaphore_signal(barrier, inc=1, device_id=plane_peer(step)[1], device_id_type=MESH)
    pl.semaphore_signal(barrier, inc=1, device_id=other, device_id_type=MESH)

    loads[0].wait()
    loads[1].wait()
    rows = jnp.concatenate([first_rows[0], first_rows[1]], axis=1)
    local_one[...] = dot_f32(rows, rows, ((0,), (0,))).reshape(PIECES, 8, FULL)
    pl.semaphore_wait(barrier, len(LINE_STEPS) + len(PLANE_STEPS) + 1)

    def reduce_all(turn, local, total, scale, meanwhile):
        def start(phase, source, target, device):
            pltpu.make_async_remote_copy(
                src_ref=source,
                dst_ref=target,
                send_sem=send_sem.at[turn, phase],
                recv_sem=recv_sem.at[turn, phase],
                device_id=device,
                device_id_type=MESH,
            ).start()

        def finish_phase(phase, buffer):
            copy = pltpu.make_async_remote_copy(
                src_ref=buffer,
                dst_ref=buffer,
                send_sem=send_sem.at[turn, phase],
                recv_sem=recv_sem.at[turn, phase],
                device_id=other,
                device_id_type=MESH,
            )
            copy.wait_recv()
            copy.wait_send()

        own_half = pl.ds(base, CHIPS)
        start(0, local.at[pl.ds(CHIPS - base, CHIPS)], half_in.at[turn], other)
        finish_phase(0, half_in.at[turn])
        half_out[turn, own_half] = local[own_half] + half_in[turn]

        for index, step in enumerate(PLANE_STEPS):
            peer, device = plane_peer(step)
            start(1, half_out.at[turn, peer], part_in.at[turn, index], device)
        meanwhile(1)
        finish_phase(1, part_in.at[turn])
        piece_out[turn] = half_out[turn, mine] + jnp.sum(part_in[turn], axis=0)

        for index, step in enumerate(LINE_STEPS):
            start(2, piece_out.at[turn], piece_in.at[turn, index], line_device(step))
        meanwhile(2)
        finish_phase(2, piece_in.at[turn])
        total[mine] = (piece_out[turn] + jnp.sum(piece_in[turn], axis=0)) * scale

        for step in PLANE_STEPS:
            start(3, total.at[mine], total.at[mine], plane_peer(step)[1])
        meanwhile(3)
        finish_phase(3, total.at[pl.ds(0, CHIPS - 1)])
        start(4, total.at[own_half], total.at[own_half], other)
        meanwhile(4)
        finish_phase(4, total.at[own_half])

    def prepare(phase):
        if phase > 1:
            return
        for side in (0, 1):
            loads[2 + side].wait()
            for mode in range(MODES):
                pair = jnp.concatenate(split(held[side, pl.ds(mode, RANK, stride=MODES), :]), axis=1)
                pairs[side, mode] = pair
                pairs_turned[side, :, mode * RANK : (mode + 1) * RANK] = pair.T

    reduce_all(0, local_one, total_one, 1.0 / 4096, prepare)
    gram = total_one[...].reshape(FULL, FULL)
    corner = jnp.concatenate(split(gram[:RANK, :RANK]), axis=1)
    column = jnp.concatenate(split(gram[:, RANK:]), axis=1)
    for mode in range(MODES):
        place = pl.ds(mode * RANK, RANK)
        pair_a, pair_b = pairs[0, mode], pairs[1, mode]
        by_a = dot_half(corner, jnp.concatenate([pair_a, pair_a], axis=0))
        by_b = dot_half(column, jnp.concatenate([pair_b, pair_b], axis=0))
        by_a = by_a[:, :RANK] + by_a[:, RANK:]
        by_b = by_b[:, :RANK] + by_b[:, RANK:]
        high, low = split(jnp.concatenate([by_a, by_b[:RANK]], axis=1))
        carried_top[0, place] = high
        carried_top[1, place] = low
        carried_low[place] = jnp.concatenate(split(by_b[RANK:]), axis=1)
    turned_a, turned_b = pairs_turned[0], pairs_turned[1]
    top = dot_half(turned_a, carried_top[0])
    top = top[:RANK] + (top[RANK:] + dot_half(turned_a[:RANK], carried_top[1]))
    low = dot_half(turned_b, carried_low[...])
    low = low[:RANK, :RANK] + (low[RANK:, :RANK] + (low[:RANK, RANK:] + low[RANK:, RANK:]))
    local_two[pl.ds(0, CHIPS)] = top.reshape(CHIPS, 8, FULL)
    local_two[pl.ds(CHIPS, CHIPS)] = jnp.concatenate([top[:, RANK:].T, low], axis=1).reshape(CHIPS, 8, FULL)
    steps = factor_steps(gram, (88, 88, 80), (factor_one, inverse_one, rest))

    def factorize(phase):
        for _ in range((0, 11, 11, 10, 0)[phase]):
            next(steps)

    reduce_all(1, local_two, total_two, 1.0 / 1048576, factorize)
    gram_two[...] = total_two[...].reshape(FULL, FULL)


def first_stage(first_a, first_b, middle_a, middle_b):
    square = jax.ShapeDtypeStruct((FULL, FULL), jnp.float32)
    vmem = pl.BlockSpec(memory_space=pltpu.VMEM)
    whole = pl.BlockSpec(memory_space=pl.ANY)
    tall = RANK * MODES
    return pl.pallas_call(
        gram_kernel,
        out_shape=(square,) * 3,
        in_specs=[whole] * 4,
        out_specs=(vmem,) * 3,
        scratch_shapes=[
            pltpu.VMEM((2, MODES, RANK), jnp.float32),
            pltpu.VMEM((2, tall, RANK), jnp.float32),
            pltpu.VMEM((PIECES, 8, FULL), jnp.float32),
            pltpu.VMEM((PIECES, 8, FULL), jnp.float32),
            pltpu.VMEM((PIECES, 8, FULL), jnp.float32),
            pltpu.VMEM((PIECES, 8, FULL), jnp.float32),
            pltpu.VMEM((2, CHIPS, 8, FULL), jnp.float32),
            pltpu.VMEM((2, PIECES, 8, FULL), jnp.float32),
            pltpu.VMEM((2, CHIPS - 1, 8, FULL), jnp.float32),
            pltpu.VMEM((2, 8, FULL), jnp.float32),
            pltpu.VMEM((2, DEPTH - 1, 8, FULL), jnp.float32),
            pltpu.VMEM((2, MODES, RANK, FULL), jnp.bfloat16),
            pltpu.VMEM((2, FULL, tall), jnp.bfloat16),
            pltpu.VMEM((2, tall, FULL), jnp.bfloat16),
            pltpu.VMEM((tall, FULL), jnp.bfloat16),
            pltpu.VMEM((FULL, FULL), jnp.float32),
            pltpu.SemaphoreType.DMA((4,)),
            pltpu.SemaphoreType.DMA((2, 5)),
            pltpu.SemaphoreType.DMA((2, 5)),
        ],
        compiler_params=pltpu.CompilerParams(
            collective_id=0, has_side_effects=True, vmem_limit_bytes=VMEM_BYTES
        ),
    )(first_a, first_b, middle_a.reshape(tall, RANK), middle_b.reshape(tall, RANK))


def finish_kernel(
    gram_two, factor_one, inverse_one, first_a, first_b, middle_a, middle_b, last_a, last_b,
    ortho_first, ortho_middle, next_core,
    first, held, carried, following, last_pairs, top_parts, low_pairs, load_sem, store_sem,
):
    loads = []
    for index, source in enumerate((first_a, first_b, middle_a, middle_b, last_a, last_b)):
        target = first.at[index] if index < 2 else held.at[index - 2]
        load = pltpu.make_async_copy(source, target, load_sem.at[index])
        load.start()
        loads.append(load)
    tall = RANK * MODES

    def pair_of(source, mode):
        return jnp.concatenate(split(held[source, pl.ds(mode, RANK, stride=MODES), :]), axis=1)

    def twice(pair):
        return jnp.concatenate([pair, pair], axis=0)

    def factor_pairs(factor):
        corner = jnp.concatenate(split(factor[:RANK, :RANK]), axis=1)
        column = jnp.concatenate(split(factor[:, RANK:]), axis=1)
        return corner, column

    def carry(pairs, block_a, block_b, target, mode):
        by_a = dot_half(pairs[0], twice(block_a))
        by_b = dot_half(pairs[1], twice(block_b))
        target[0, pl.ds(mode, RANK, stride=MODES)] = by_a[:, :RANK] + by_a[:, RANK:]
        target[1, pl.ds(mode, FULL, stride=MODES)] = by_b[:, :RANK] + by_b[:, RANK:]

    stores = []

    def send(buffer, target, part):
        for side in (0, 1):
            store = pltpu.make_async_copy(
                buffer.at[side, part], target.at[part, pl.ds(side * RANK, RANK)], store_sem.at[len(stores)]
            )
            store.start()
            stores.append(store)

    pairs_one = factor_pairs(factor_one[...])

    def begin():
        for load in loads[:4]:
            load.wait()
        first_rows = jnp.concatenate([first[0], first[1]], axis=1)
        ortho_first[...] = dot_f32(first_rows, inverse_one[...], ((1,), (1,)))
        zero = jnp.zeros((tall, RANK), jnp.float32)
        carried[0, pl.ds(tall, tall)] = zero
        following[0, pl.ds(tall, tall)] = zero

    def carry_middle(mode):
        carry(pairs_one, pair_of(0, mode), pair_of(1, mode), carried, mode)

    def prepare_last(mode):
        if mode == 0:
            loads[4].wait()
            loads[5].wait()
        last_pairs[0, mode] = pair_of(2, mode)
        last_pairs[1, mode] = pair_of(3, mode)

    chunk = 512

    def prepare_rows(start):
        part = pl.ds(start, chunk)
        high, low = split(jnp.concatenate([carried[0, part], carried[1, part]], axis=1))
        top_parts[0, part] = high
        top_parts[1, part] = low
        low_pairs[part] = jnp.concatenate(split(carried[1, pl.ds(tall + start, chunk)]), axis=1)

    tasks = [begin]
    tasks += [lambda mode=mode: carry_middle(mode) for mode in range(MODES)]
    tasks += [lambda start=start: prepare_rows(start) for start in range(0, tall, chunk)]
    tasks += [lambda mode=mode: (prepare_last(mode), prepare_last(mode + 1)) for mode in range(0, MODES, 2)]
    steps = factor_steps(gram_two[...], (64, 64, 64, 64))
    for index in range(FULL // 8):
        next(steps)
        if 2 <= index < 2 + len(tasks):
            tasks[index - 2]()
    factor_two, inverse_two = next(steps)

    pairs_two = factor_pairs(factor_two)
    for mode in range(MODES):
        carry(pairs_two, last_pairs[0, mode], last_pairs[1, mode], following, mode)
    send(following, next_core, pl.ds(0, FULL * MODES))
    inverse = inverse_two.T
    high, low = split(inverse)
    corner = twice(jnp.concatenate([high[RANK:, RANK:], low[RANK:, RANK:]], axis=1))
    for start in range(0, tall, chunk):
        part = pl.ds(start, chunk)
        result = dot_half(top_parts[0, part], high) + (
            dot_half(top_parts[1, part], high) + dot_half(top_parts[0, part], low)
        )
        carried[0, part] = result[:, :RANK]
        carried[1, part] = result[:, RANK:]
        send(carried, ortho_middle, part)
    for start in range(0, tall, chunk):
        result = dot_half(low_pairs[pl.ds(start, chunk)], corner)
        part = pl.ds(tall + start, chunk)
        carried[1, part] = result[:, :RANK] + result[:, RANK:]
        send(carried, ortho_middle, part)
    for store in stores:
        store.wait()


def finish(gram_two, factor_one, inverse_one, first_a, first_b, *blocks):
    vmem = pl.BlockSpec(memory_space=pltpu.VMEM)
    whole = pl.BlockSpec(memory_space=pl.ANY)
    rows, tall = FULL * MODES, RANK * MODES
    flat = [block.reshape(tall, RANK) for block in blocks]
    ortho_first, ortho_middle, next_core = pl.pallas_call(
        finish_kernel,
        out_shape=(
            jax.ShapeDtypeStruct((MODES, FULL), jnp.float32),
            jax.ShapeDtypeStruct((rows, FULL), jnp.float32),
            jax.ShapeDtypeStruct((rows, FULL), jnp.float32),
        ),
        in_specs=[vmem] * 3 + [whole] * 6,
        out_specs=(vmem, whole, whole),
        scratch_shapes=[
            pltpu.VMEM((2, MODES, RANK), jnp.float32),
            pltpu.VMEM((4, tall, RANK), jnp.float32),
            pltpu.VMEM((2, rows, RANK), jnp.float32),
            pltpu.VMEM((2, rows, RANK), jnp.float32),
            pltpu.VMEM((2, MODES, RANK, FULL), jnp.bfloat16),
            pltpu.VMEM((2, tall, FULL), jnp.bfloat16),
            pltpu.VMEM((tall, FULL), jnp.bfloat16),
            pltpu.SemaphoreType.DMA((6,)),
            pltpu.SemaphoreType.DMA((18,)),
        ],
        compiler_params=pltpu.CompilerParams(vmem_limit_bytes=VMEM_BYTES),
    )(gram_two, factor_one, inverse_one, first_a, first_b, *flat)
    shape = (FULL, MODES, FULL)
    return ortho_first, ortho_middle.reshape(shape), next_core.reshape(shape)


def body(first_a, first_b, middle_a, middle_b, last_a, last_b):
    gram_two, factor_one, inverse_one = first_stage(first_a, first_b, middle_a, middle_b)
    return finish(gram_two, factor_one, inverse_one, first_a, first_b, middle_a, middle_b, last_a, last_b)


def solution(mesh):
    placed = (
        P(("wide", "narrow"), None),
        P(("wide", "narrow"), None),
        P(None, ("wide", "narrow"), None),
        P(None, ("wide", "narrow"), None),
        P(None, ("wide", "narrow"), None),
        P(None, ("wide", "narrow"), None),
    )
    return jax.shard_map(
        body,
        mesh=mesh,
        in_specs=placed,
        out_specs=(
            P(("wide", "narrow"), None),
            P(None, ("wide", "narrow"), None),
            P(None, ("wide", "narrow"), None),
        ),
        check_vma=False,
    )
```

```python
import jax
import jax.numpy as jnp
from jax import lax
from jax.experimental import pallas as pl
from jax.experimental.pallas import tpu as pltpu
from jax.sharding import PartitionSpec as P

MESH = pl.DeviceIdType.MESH
HIGHEST_PRECISION = lax.Precision.HIGHEST
PIECES = 32
CHIPS = 16
SIDE = 4
DEPTH = 8
RANK = 128
FULL = 256
MODES = 16
VMEM_BYTES = 60 * 1024 * 1024


def dot_f32(left, right, dims):
    return lax.dot_general(
        left, right, (dims, ((), ())), precision=HIGHEST_PRECISION, preferred_element_type=jnp.float32
    )


def far_first(offsets, sizes):
    def hops(offset):
        return sum(min(step, size - step) for step, size in zip(offset, sizes))

    return sorted((offset for offset in offsets if any(offset)), key=lambda offset: -hops(offset))


PLANE_STEPS = far_first([(x, y) for x in range(SIDE) for y in range(SIDE)], (SIDE, SIDE))
LINE_STEPS = far_first([(z,) for z in range(DEPTH)], (DEPTH,))


def split(value):
    high = value.astype(jnp.bfloat16)
    return high, (value - high.astype(jnp.float32)).astype(jnp.bfloat16)


def dot_half(left, right):
    return jnp.dot(left, right, preferred_element_type=jnp.float32)


def factor_steps(square, widths, block, refs=None):
    rest = square
    start = 0
    uppers, lowers = [], []
    for panel_rows in widths:
        stop = start + panel_rows
        if refs is not None and start:
            rest = refs[2][pl.ds(start, FULL - start), :]
        halves = [rest[:panel_rows, :128], rest[:panel_rows, 128:]]
        below = rest[panel_rows:]
        done = []
        for base in range(start, stop, block):
            side, lane = base // 128, base % 128
            height = stop - base
            lanes = lax.broadcasted_iota(jnp.int32, (height, 128), 1)
            rows = lax.broadcasted_iota(jnp.int32, (height, 128), 0)
            columns = [
                jnp.broadcast_to(halves[side][:, lane + t : lane + t + 1], (height, 128)) for t in range(block)
            ]
            inside = (lanes >= lane) & (lanes < lane + block)
            halves[side] = jnp.where(inside, jnp.where(lanes == rows + lane, 1.0, 0.0), halves[side])
            for t in range(block):
                inverse = 1.0 / columns[t][t : t + 1]
                column = jnp.where(rows > t, columns[t], 0.0)
                factors = column * inverse
                for later in range(t + 1, block):
                    entry = columns[later][t : t + 1]
                    taken = (column * entry) * inverse if later == t + 1 else factors * entry
                    columns[later] = columns[later] - taken
                halves = [half - factors * half[t : t + 1] for half in halves]
            small, small_lanes = rows[:block], lanes[:block]
            pivots, top = columns[0][:block], halves[side][:block]
            for t in range(block):
                pivots = jnp.where(small == t, columns[t][:block], pivots)
                top = jnp.where(small_lanes == lane + t, columns[t][:block], top)
            root = lax.rsqrt(pivots)
            ready = [half[:block] * root for half in halves]
            done.append(jnp.concatenate(ready, axis=1))
            top = top * root
            upper = [top, ready[1]] if side == 0 else [ready[0], top]
            row = small + base
            uppers.append(
                jnp.concatenate([jnp.where(small_lanes + 128 * s >= row, upper[s], 0.0) for s in (0, 1)], axis=1)
            )
            lowers.append(
                jnp.concatenate([jnp.where(small_lanes + 128 * s <= row, ready[s], 0.0) for s in (0, 1)], axis=1)
            )
            halves = [half[block:] for half in halves]
            if base + block == stop and stop < FULL:
                done = jnp.concatenate(done, axis=0)
                row_index = lax.broadcasted_iota(jnp.int32, (panel_rows, FULL), 0) + start
                lane_index = lax.broadcasted_iota(jnp.int32, (panel_rows, FULL), 1)
                right = jnp.where((lane_index > row_index) & (lane_index < stop), 0.0, done)
                low = stop // 128 * 128
                update = dot_f32(done[:, low:], right, ((0,), (0,)))[stop - low :]
                below_lanes = lax.broadcasted_iota(jnp.int32, below.shape, 1)
                rest = jnp.where((below_lanes >= start) & (below_lanes < stop), 0.0, below) - update
                if refs is not None:
                    refs[2][pl.ds(stop, FULL - stop), :] = rest
            if refs is not None:
                refs[0][pl.ds(base, block), :] = uppers.pop()
                refs[1][pl.ds(base, block), :] = lowers.pop()
            yield
        start = stop
    yield jnp.concatenate(uppers, axis=0), jnp.concatenate(lowers, axis=0)


def gram_kernel(
    first_a, first_b, middle_a, middle_b, gram_two, factor_one, inverse_one,
    first_rows, held, local_one, local_two, total_one, total_two,
    half_in, half_out, part_in, piece_out, piece_in, pairs, pairs_turned, carried_top, carried_low, rest,
    load_sem, send_sem, recv_sem,
):
    wide = lax.axis_index("wide")
    core = lax.axis_index("narrow")
    spot_x = wide // 32
    spot_z = (wide // 4) % 8
    spot_y = wide % 4
    mine = core * CHIPS + spot_x * SIDE + spot_y
    base = core * CHIPS
    other = (wide, 1 - core)

    def plane_peer(step):
        x, y = (spot_x + step[0]) % SIDE, (spot_y + step[1]) % SIDE
        return base + x * SIDE + y, (x * 32 + spot_z * 4 + y, core)

    def line_device(step):
        return (spot_x * 32 + ((spot_z + step[0]) % DEPTH) * 4 + spot_y, core)

    loads = []
    for index, (source, target) in enumerate(
        ((first_a, first_rows.at[0]), (first_b, first_rows.at[1]), (middle_a, held.at[0]), (middle_b, held.at[1]))
    ):
        load = pltpu.make_async_copy(source, target, load_sem.at[index])
        load.start()
        loads.append(load)

    barrier = pltpu.get_barrier_semaphore()
    for step in LINE_STEPS:
        pl.semaphore_signal(barrier, inc=1, device_id=line_device(step), device_id_type=MESH)
    for step in PLANE_STEPS:
        pl.semaphore_signal(barrier, inc=1, device_id=plane_peer(step)[1], device_id_type=MESH)
    pl.semaphore_signal(barrier, inc=1, device_id=other, device_id_type=MESH)

    loads[0].wait()
    loads[1].wait()
    rows = jnp.concatenate([first_rows[0], first_rows[1]], axis=1)
    local_one[...] = dot_f32(rows, rows, ((0,), (0,))).reshape(PIECES, 8, FULL)
    pl.semaphore_wait(barrier, len(LINE_STEPS) + len(PLANE_STEPS) + 1)

    def reduce_all(turn, local, total, scale, meanwhile):
        def start(phase, source, target, device):
            pltpu.make_async_remote_copy(
                src_ref=source,
                dst_ref=target,
                send_sem=send_sem.at[turn, phase],
                recv_sem=recv_sem.at[turn, phase],
                device_id=device,
                device_id_type=MESH,
            ).start()

        def finish_phase(phase, buffer):
            copy = pltpu.make_async_remote_copy(
                src_ref=buffer,
                dst_ref=buffer,
                send_sem=send_sem.at[turn, phase],
                recv_sem=recv_sem.at[turn, phase],
                device_id=other,
                device_id_type=MESH,
            )
            copy.wait_recv()
            copy.wait_send()

        own_half = pl.ds(base, CHIPS)
        start(0, local.at[pl.ds(CHIPS - base, CHIPS)], half_in.at[turn], other)
        finish_phase(0, half_in.at[turn])
        half_out[turn, own_half] = local[own_half] + half_in[turn]

        for index, step in enumerate(PLANE_STEPS):
            peer, device = plane_peer(step)
            start(1, half_out.at[turn, peer], part_in.at[turn, index], device)
        meanwhile(1)
        finish_phase(1, part_in.at[turn])
        piece_out[turn] = half_out[turn, mine] + jnp.sum(part_in[turn], axis=0)

        for index, step in enumerate(LINE_STEPS):
            start(2, piece_out.at[turn], piece_in.at[turn, index], line_device(step))
        meanwhile(2)
        finish_phase(2, piece_in.at[turn])
        total[mine] = (piece_out[turn] + jnp.sum(piece_in[turn], axis=0)) * scale

        for step in PLANE_STEPS:
            start(3, total.at[mine], total.at[mine], plane_peer(step)[1])
        meanwhile(3)
        finish_phase(3, total.at[pl.ds(0, CHIPS - 1)])
        start(4, total.at[own_half], total.at[own_half], other)
        meanwhile(4)
        finish_phase(4, total.at[own_half])

    def prepare(phase):
        if phase > 1:
            return
        for side in (0, 1):
            loads[2 + side].wait()
            for mode in range(MODES):
                pair = jnp.concatenate(split(held[side, pl.ds(mode, RANK, stride=MODES), :]), axis=1)
                pairs[side, mode] = pair
                pairs_turned[side, :, mode * RANK : (mode + 1) * RANK] = pair.T

    reduce_all(0, local_one, total_one, 1.0 / 4096, prepare)
    gram = total_one[...].reshape(FULL, FULL)
    corner = jnp.concatenate(split(gram[:RANK, :RANK]), axis=1)
    column = jnp.concatenate(split(gram[:, RANK:]), axis=1)
    for mode in range(MODES):
        place = pl.ds(mode * RANK, RANK)
        pair_a, pair_b = pairs[0, mode], pairs[1, mode]
        by_a = dot_half(corner, jnp.concatenate([pair_a, pair_a], axis=0))
        by_b = dot_half(column, jnp.concatenate([pair_b, pair_b], axis=0))
        by_a = by_a[:, :RANK] + by_a[:, RANK:]
        by_b = by_b[:, :RANK] + by_b[:, RANK:]
        high, low = split(jnp.concatenate([by_a, by_b[:RANK]], axis=1))
        carried_top[0, place] = high
        carried_top[1, place] = low
        carried_low[place] = jnp.concatenate(split(by_b[RANK:]), axis=1)
    turned_a, turned_b = pairs_turned[0], pairs_turned[1]
    top = dot_half(turned_a, carried_top[0])
    top = top[:RANK] + (top[RANK:] + dot_half(turned_a[:RANK], carried_top[1]))
    low = dot_half(turned_b, carried_low[...])
    low = low[:RANK, :RANK] + (low[RANK:, :RANK] + (low[:RANK, RANK:] + low[RANK:, RANK:]))
    local_two[pl.ds(0, CHIPS)] = top.reshape(CHIPS, 8, FULL)
    local_two[pl.ds(CHIPS, CHIPS)] = jnp.concatenate([top[:, RANK:].T, low], axis=1).reshape(CHIPS, 8, FULL)
    steps = factor_steps(gram, (88, 88, 80), 8, (factor_one, inverse_one, rest))

    def factorize(phase):
        for _ in range((0, 11, 11, 10, 0)[phase]):
            next(steps)

    reduce_all(1, local_two, total_two, 1.0 / 1048576, factorize)
    gram_two[...] = total_two[...].reshape(FULL, FULL)


def first_stage(first_a, first_b, middle_a, middle_b):
    square = jax.ShapeDtypeStruct((FULL, FULL), jnp.float32)
    vmem = pl.BlockSpec(memory_space=pltpu.VMEM)
    whole = pl.BlockSpec(memory_space=pl.ANY)
    tall = RANK * MODES
    return pl.pallas_call(
        gram_kernel,
        out_shape=(square,) * 3,
        in_specs=[whole] * 4,
        out_specs=(vmem,) * 3,
        scratch_shapes=[
            pltpu.VMEM((2, MODES, RANK), jnp.float32),
            pltpu.VMEM((2, tall, RANK), jnp.float32),
            pltpu.VMEM((PIECES, 8, FULL), jnp.float32),
            pltpu.VMEM((PIECES, 8, FULL), jnp.float32),
            pltpu.VMEM((PIECES, 8, FULL), jnp.float32),
            pltpu.VMEM((PIECES, 8, FULL), jnp.float32),
            pltpu.VMEM((2, CHIPS, 8, FULL), jnp.float32),
            pltpu.VMEM((2, PIECES, 8, FULL), jnp.float32),
            pltpu.VMEM((2, CHIPS - 1, 8, FULL), jnp.float32),
            pltpu.VMEM((2, 8, FULL), jnp.float32),
            pltpu.VMEM((2, DEPTH - 1, 8, FULL), jnp.float32),
            pltpu.VMEM((2, MODES, RANK, FULL), jnp.bfloat16),
            pltpu.VMEM((2, FULL, tall), jnp.bfloat16),
            pltpu.VMEM((2, tall, FULL), jnp.bfloat16),
            pltpu.VMEM((tall, FULL), jnp.bfloat16),
            pltpu.VMEM((FULL, FULL), jnp.float32),
            pltpu.SemaphoreType.DMA((4,)),
            pltpu.SemaphoreType.DMA((2, 5)),
            pltpu.SemaphoreType.DMA((2, 5)),
        ],
        compiler_params=pltpu.CompilerParams(
            collective_id=0, has_side_effects=True, vmem_limit_bytes=VMEM_BYTES
        ),
    )(first_a, first_b, middle_a.reshape(tall, RANK), middle_b.reshape(tall, RANK))


def finish_kernel(
    gram_two, factor_one, inverse_one, first_a, first_b, middle_a, middle_b, last_a, last_b,
    ortho_first, ortho_middle, next_core,
    zeros, first, held, carried, following, last_pairs, top_parts, low_pairs, load_sem, store_sem,
):
    loads = []
    for index, source in enumerate((first_a, first_b, middle_a, middle_b, last_a, last_b)):
        target = first.at[index] if index < 2 else held.at[index - 2]
        load = pltpu.make_async_copy(source, target, load_sem.at[index])
        load.start()
        loads.append(load)
    tall = RANK * MODES

    def pair_of(source, mode):
        return jnp.concatenate(split(held[source, pl.ds(mode, RANK, stride=MODES), :]), axis=1)

    def twice(pair):
        return jnp.concatenate([pair, pair], axis=0)

    def factor_pairs(factor):
        corner = jnp.concatenate(split(factor[:RANK, :RANK]), axis=1)
        column = jnp.concatenate(split(factor[:, RANK:]), axis=1)
        return corner, column

    def carry(pairs, block_a, block_b, target, mode):
        by_a = dot_half(pairs[0], twice(block_a))
        by_b = dot_half(pairs[1], twice(block_b))
        by_a = by_a[:, :RANK] + by_a[:, RANK:]
        by_b = by_b[:, :RANK] + by_b[:, RANK:]
        if target is carried:
            target[0, pl.ds(mode, RANK, stride=MODES)] = by_a
            target[1, pl.ds(mode, FULL, stride=MODES)] = by_b
        else:
            target[0, pl.ds(mode * RANK, RANK)] = by_a
            target[1, pl.ds(mode * FULL, FULL)] = by_b
            start_store(target.at[0, pl.ds(mode * RANK, RANK)], next_core.at[pl.ds(0, RANK), mode, pl.ds(0, RANK)])
            start_store(target.at[1, pl.ds(mode * FULL, FULL)], next_core.at[:, mode, pl.ds(RANK, RANK)])

    stores = []

    def start_store(source, target):
        store = pltpu.make_async_copy(source, target, store_sem.at[len(stores)])
        store.start()
        stores.append(store)

    def send(buffer, target, part):
        for side in (0, 1):
            store = pltpu.make_async_copy(
                buffer.at[side, part], target.at[part, pl.ds(side * RANK, RANK)], store_sem.at[len(stores)]
            )
            store.start()
            stores.append(store)

    pairs_one = factor_pairs(factor_one[...])

    def begin():
        for load in loads[:4]:
            load.wait()
        first_rows = jnp.concatenate([first[0], first[1]], axis=1)
        ortho_first[...] = dot_f32(first_rows, inverse_one[...], ((1,), (1,)))
        zero = jnp.zeros((tall, RANK), jnp.float32)
        carried[0, pl.ds(tall, tall)] = zero
        zeros[...] = jnp.zeros_like(zeros)
        start_store(zeros, next_core.at[pl.ds(RANK, RANK), :, pl.ds(0, RANK)])
        start_store(carried.at[0, pl.ds(tall, tall)], ortho_middle.at[pl.ds(tall, tall), pl.ds(0, RANK)])

    def carry_middle(mode):
        carry(pairs_one, pair_of(0, mode), pair_of(1, mode), carried, mode)

    def prepare_last(mode):
        if mode == 0:
            loads[4].wait()
            loads[5].wait()
        last_pairs[0, mode] = pair_of(2, mode)
        last_pairs[1, mode] = pair_of(3, mode)

    chunk = 512

    def prepare_rows(start):
        part = pl.ds(start, chunk)
        high, low = split(jnp.concatenate([carried[0, part], carried[1, part]], axis=1))
        top_parts[0, part] = high
        top_parts[1, part] = low
        low_pairs[part] = jnp.concatenate(split(carried[1, pl.ds(tall + start, chunk)]), axis=1)

    tasks = [begin]
    tasks += [lambda mode=mode: carry_middle(mode) for mode in range(MODES)]
    tasks += [lambda start=start: prepare_rows(start) for start in range(0, tall, chunk)]
    tasks += [lambda mode=mode: (prepare_last(mode), prepare_last(mode + 1)) for mode in range(0, MODES, 2)]
    steps = factor_steps(gram_two[...], (64, 64, 64, 64), 16)
    for index in range(FULL // 16):
        next(steps)
        for task in tasks[2 * index - 2 : 2 * index] if index else []:
            task()
    factor_two, inverse_two = next(steps)

    pairs_two = factor_pairs(factor_two)
    for mode in range(MODES):
        carry(pairs_two, last_pairs[0, mode], last_pairs[1, mode], following, mode)
    inverse = inverse_two.T
    high, low = split(inverse)
    corner = twice(jnp.concatenate([high[RANK:, RANK:], low[RANK:, RANK:]], axis=1))
    for start in range(0, tall, chunk):
        part = pl.ds(start, chunk)
        result = dot_half(top_parts[0, part], high) + (
            dot_half(top_parts[1, part], high) + dot_half(top_parts[0, part], low)
        )
        carried[0, part] = result[:, :RANK]
        carried[1, part] = result[:, RANK:]
        send(carried, ortho_middle, part)
    for start in range(0, tall, chunk):
        result = dot_half(low_pairs[pl.ds(start, chunk)], corner)
        part = pl.ds(tall + start, chunk)
        carried[1, part] = result[:, :RANK] + result[:, RANK:]
        start_store(carried.at[1, part], ortho_middle.at[part, pl.ds(RANK, RANK)])
    for store in stores:
        store.wait()


def finish(gram_two, factor_one, inverse_one, first_a, first_b, *blocks):
    vmem = pl.BlockSpec(memory_space=pltpu.VMEM)
    whole = pl.BlockSpec(memory_space=pl.ANY)
    rows, tall = FULL * MODES, RANK * MODES
    flat = [block.reshape(tall, RANK) for block in blocks]
    ortho_first, ortho_middle, next_core = pl.pallas_call(
        finish_kernel,
        out_shape=(
            jax.ShapeDtypeStruct((MODES, FULL), jnp.float32),
            jax.ShapeDtypeStruct((rows, FULL), jnp.float32),
            jax.ShapeDtypeStruct((FULL, MODES, FULL), jnp.float32),
        ),
        in_specs=[vmem] * 3 + [whole] * 6,
        out_specs=(vmem, whole, whole),
        scratch_shapes=[
            pltpu.VMEM((RANK, MODES, RANK), jnp.float32),
            pltpu.VMEM((2, MODES, RANK), jnp.float32),
            pltpu.VMEM((4, tall, RANK), jnp.float32),
            pltpu.VMEM((2, rows, RANK), jnp.float32),
            pltpu.VMEM((2, rows, RANK), jnp.float32),
            pltpu.VMEM((2, MODES, RANK, FULL), jnp.bfloat16),
            pltpu.VMEM((2, tall, FULL), jnp.bfloat16),
            pltpu.VMEM((tall, FULL), jnp.bfloat16),
            pltpu.SemaphoreType.DMA((6,)),
            pltpu.SemaphoreType.DMA((64,)),
        ],
        compiler_params=pltpu.CompilerParams(vmem_limit_bytes=VMEM_BYTES),
    )(gram_two, factor_one, inverse_one, first_a, first_b, *flat)
    shape = (FULL, MODES, FULL)
    return ortho_first, ortho_middle.reshape(shape), next_core.reshape(shape)


def body(first_a, first_b, middle_a, middle_b, last_a, last_b):
    gram_two, factor_one, inverse_one = first_stage(first_a, first_b, middle_a, middle_b)
    return finish(gram_two, factor_one, inverse_one, first_a, first_b, middle_a, middle_b, last_a, last_b)


def solution(mesh):
    placed = (
        P(("wide", "narrow"), None),
        P(("wide", "narrow"), None),
        P(None, ("wide", "narrow"), None),
        P(None, ("wide", "narrow"), None),
        P(None, ("wide", "narrow"), None),
        P(None, ("wide", "narrow"), None),
    )
    return jax.shard_map(
        body,
        mesh=mesh,
        in_specs=placed,
        out_specs=(
            P(("wide", "narrow"), None),
            P(None, ("wide", "narrow"), None),
            P(None, ("wide", "narrow"), None),
        ),
        check_vma=False,
    )
```

```python
import jax
import jax.numpy as jnp
from jax import lax
from jax.experimental import pallas as pl
from jax.experimental.pallas import tpu as pltpu
from jax.sharding import PartitionSpec as P

MESH = pl.DeviceIdType.MESH
HIGHEST_PRECISION = lax.Precision.HIGHEST
PIECES = 32
CHIPS = 16
SIDE = 4
DEPTH = 8
RANK = 128
FULL = 256
MODES = 16
VMEM_BYTES = 60 * 1024 * 1024


def dot_f32(left, right, dims):
    return lax.dot_general(
        left, right, (dims, ((), ())), precision=HIGHEST_PRECISION, preferred_element_type=jnp.float32
    )


def far_first(offsets, sizes):
    def hops(offset):
        return sum(min(step, size - step) for step, size in zip(offset, sizes))

    return sorted((offset for offset in offsets if any(offset)), key=lambda offset: -hops(offset))


PLANE_STEPS = far_first([(x, y) for x in range(SIDE) for y in range(SIDE)], (SIDE, SIDE))
LINE_STEPS = far_first([(z,) for z in range(DEPTH)], (DEPTH,))


def split(value):
    high = value.astype(jnp.bfloat16)
    return high, (value - high.astype(jnp.float32)).astype(jnp.bfloat16)


def dot_half(left, right):
    return jnp.dot(left, right, preferred_element_type=jnp.float32)


def factor_steps(square, widths, block, refs=None):
    rest = square
    start = 0
    uppers, lowers = [], []
    for panel_rows in widths:
        stop = start + panel_rows
        if refs is not None and start:
            rest = refs[2][pl.ds(start, FULL - start), :]
        halves = [rest[:panel_rows, :128], rest[:panel_rows, 128:]]
        below = rest[panel_rows:]
        done = []
        for base in range(start, stop, block):
            side, lane = base // 128, base % 128
            height = stop - base
            lanes = lax.broadcasted_iota(jnp.int32, (height, 128), 1)
            rows = lax.broadcasted_iota(jnp.int32, (height, 128), 0)
            columns = [
                jnp.broadcast_to(halves[side][:, lane + t : lane + t + 1], (height, 128)) for t in range(block)
            ]
            inside = (lanes >= lane) & (lanes < lane + block)
            halves[side] = jnp.where(inside, jnp.where(lanes == rows + lane, 1.0, 0.0), halves[side])
            for t in range(block):
                inverse = 1.0 / columns[t][t : t + 1]
                column = jnp.where(rows > t, columns[t], 0.0)
                factors = column * inverse
                for later in range(t + 1, block):
                    entry = columns[later][t : t + 1]
                    taken = (column * entry) * inverse if later == t + 1 else factors * entry
                    columns[later] = columns[later] - taken
                halves = [half - factors * half[t : t + 1] for half in halves]
            small, small_lanes = rows[:block], lanes[:block]
            pivots, top = columns[0][:block], halves[side][:block]
            for t in range(block):
                pivots = jnp.where(small == t, columns[t][:block], pivots)
                top = jnp.where(small_lanes == lane + t, columns[t][:block], top)
            root = lax.rsqrt(pivots)
            ready = [half[:block] * root for half in halves]
            done.append(jnp.concatenate(ready, axis=1))
            top = top * root
            upper = [top, ready[1]] if side == 0 else [ready[0], top]
            row = small + base
            uppers.append(
                jnp.concatenate([jnp.where(small_lanes + 128 * s >= row, upper[s], 0.0) for s in (0, 1)], axis=1)
            )
            lowers.append(
                jnp.concatenate([jnp.where(small_lanes + 128 * s <= row, ready[s], 0.0) for s in (0, 1)], axis=1)
            )
            halves = [half[block:] for half in halves]
            if base + block == stop and stop < FULL:
                done = jnp.concatenate(done, axis=0)
                row_index = lax.broadcasted_iota(jnp.int32, (panel_rows, FULL), 0) + start
                lane_index = lax.broadcasted_iota(jnp.int32, (panel_rows, FULL), 1)
                right = jnp.where((lane_index > row_index) & (lane_index < stop), 0.0, done)
                low = stop // 128 * 128
                update = dot_f32(done[:, low:], right, ((0,), (0,)))[stop - low :]
                below_lanes = lax.broadcasted_iota(jnp.int32, below.shape, 1)
                rest = jnp.where((below_lanes >= start) & (below_lanes < stop), 0.0, below) - update
                if refs is not None:
                    refs[2][pl.ds(stop, FULL - stop), :] = rest
            if refs is not None:
                refs[0][pl.ds(base, block), :] = uppers.pop()
                refs[1][pl.ds(base, block), :] = lowers.pop()
            yield
        start = stop
    yield jnp.concatenate(uppers, axis=0), jnp.concatenate(lowers, axis=0)


def gram_kernel(
    first_a, first_b, middle_a, middle_b, gram_two, factor_one, inverse_one,
    first_rows, held, local_one, local_two, total_one, total_two,
    half_in, half_out, part_in, piece_out, piece_in, pairs, pairs_turned, carried_top, carried_low, rest, factor_held, inverse_held,
    out_sem, load_sem, send_sem, recv_sem,
):
    wide = lax.axis_index("wide")
    core = lax.axis_index("narrow")
    spot_x = wide // 32
    spot_z = (wide // 4) % 8
    spot_y = wide % 4
    mine = core * CHIPS + spot_x * SIDE + spot_y
    base = core * CHIPS
    other = (wide, 1 - core)

    def plane_peer(step):
        x, y = (spot_x + step[0]) % SIDE, (spot_y + step[1]) % SIDE
        return base + x * SIDE + y, (x * 32 + spot_z * 4 + y, core)

    def line_device(step):
        return (spot_x * 32 + ((spot_z + step[0]) % DEPTH) * 4 + spot_y, core)

    loads = []
    for index, (source, target) in enumerate(
        ((first_a, first_rows.at[0]), (first_b, first_rows.at[1]), (middle_a, held.at[0]), (middle_b, held.at[1]))
    ):
        load = pltpu.make_async_copy(source, target, load_sem.at[index])
        load.start()
        loads.append(load)

    barrier = pltpu.get_barrier_semaphore()
    for step in LINE_STEPS:
        pl.semaphore_signal(barrier, inc=1, device_id=line_device(step), device_id_type=MESH)
    for step in PLANE_STEPS:
        pl.semaphore_signal(barrier, inc=1, device_id=plane_peer(step)[1], device_id_type=MESH)
    pl.semaphore_signal(barrier, inc=1, device_id=other, device_id_type=MESH)

    loads[0].wait()
    loads[1].wait()
    rows = jnp.concatenate([first_rows[0], first_rows[1]], axis=1)
    local_one[...] = dot_f32(rows, rows, ((0,), (0,))).reshape(PIECES, 8, FULL)
    pl.semaphore_wait(barrier, len(LINE_STEPS) + len(PLANE_STEPS) + 1)

    def reduce_all(turn, local, total, scale, meanwhile):
        def start(phase, source, target, device):
            pltpu.make_async_remote_copy(
                src_ref=source,
                dst_ref=target,
                send_sem=send_sem.at[turn, phase],
                recv_sem=recv_sem.at[turn, phase],
                device_id=device,
                device_id_type=MESH,
            ).start()

        def finish_phase(phase, buffer):
            copy = pltpu.make_async_remote_copy(
                src_ref=buffer,
                dst_ref=buffer,
                send_sem=send_sem.at[turn, phase],
                recv_sem=recv_sem.at[turn, phase],
                device_id=other,
                device_id_type=MESH,
            )
            copy.wait_recv()
            copy.wait_send()

        own_half = pl.ds(base, CHIPS)
        start(0, local.at[pl.ds(CHIPS - base, CHIPS)], half_in.at[turn], other)
        finish_phase(0, half_in.at[turn])
        half_out[turn, own_half] = local[own_half] + half_in[turn]

        for index, step in enumerate(PLANE_STEPS):
            peer, device = plane_peer(step)
            start(1, half_out.at[turn, peer], part_in.at[turn, index], device)
        meanwhile(1)
        finish_phase(1, part_in.at[turn])
        piece_out[turn] = half_out[turn, mine] + jnp.sum(part_in[turn], axis=0)

        for index, step in enumerate(LINE_STEPS):
            start(2, piece_out.at[turn], piece_in.at[turn, index], line_device(step))
        meanwhile(2)
        finish_phase(2, piece_in.at[turn])
        total[mine] = (piece_out[turn] + jnp.sum(piece_in[turn], axis=0)) * scale

        for step in PLANE_STEPS:
            start(3, total.at[mine], total.at[mine], plane_peer(step)[1])
        meanwhile(3)
        finish_phase(3, total.at[pl.ds(0, CHIPS - 1)])
        start(4, total.at[own_half], total.at[own_half], other)
        meanwhile(4)
        finish_phase(4, total.at[own_half])

    def prepare(phase):
        if phase > 1:
            return
        for side in (0, 1):
            loads[2 + side].wait()
            for mode in range(MODES):
                pair = jnp.concatenate(split(held[side, pl.ds(mode, RANK, stride=MODES), :]), axis=1)
                pairs[side, mode] = pair
                pairs_turned[side, :, mode * RANK : (mode + 1) * RANK] = pair.T

    reduce_all(0, local_one, total_one, 1.0 / 4096, prepare)
    gram = total_one[...].reshape(FULL, FULL)
    corner = jnp.concatenate(split(gram[:RANK, :RANK]), axis=1)
    column = jnp.concatenate(split(gram[:, RANK:]), axis=1)
    for mode in range(MODES):
        place = pl.ds(mode * RANK, RANK)
        pair_a, pair_b = pairs[0, mode], pairs[1, mode]
        by_a = dot_half(corner, jnp.concatenate([pair_a, pair_a], axis=0))
        by_b = dot_half(column, jnp.concatenate([pair_b, pair_b], axis=0))
        by_a = by_a[:, :RANK] + by_a[:, RANK:]
        by_b = by_b[:, :RANK] + by_b[:, RANK:]
        high, low = split(jnp.concatenate([by_a, by_b[:RANK]], axis=1))
        carried_top[0, place] = high
        carried_top[1, place] = low
        carried_low[place] = jnp.concatenate(split(by_b[RANK:]), axis=1)
    turned_a, turned_b = pairs_turned[0], pairs_turned[1]
    top = dot_half(turned_a, carried_top[0])
    top = top[:RANK] + (top[RANK:] + dot_half(turned_a[:RANK], carried_top[1]))
    low = dot_half(turned_b, carried_low[...])
    low = low[:RANK, :RANK] + (low[RANK:, :RANK] + (low[:RANK, RANK:] + low[RANK:, RANK:]))
    local_two[pl.ds(0, CHIPS)] = top.reshape(CHIPS, 8, FULL)
    local_two[pl.ds(CHIPS, CHIPS)] = jnp.concatenate([top[:, RANK:].T, low], axis=1).reshape(CHIPS, 8, FULL)
    steps = factor_steps(gram, (88, 88, 80), 8, (factor_held, inverse_held, rest))

    outs = [
        pltpu.make_async_copy(source, target, out_sem.at[index])
        for index, (source, target) in enumerate(((factor_held, factor_one), (inverse_held, inverse_one)))
    ]

    def factorize(phase):
        for _ in range((0, 11, 11, 10, 0)[phase]):
            next(steps)
        if phase == 4:
            for out in outs:
                out.start()

    reduce_all(1, local_two, total_two, 1.0 / 1048576, factorize)
    gram_two[...] = total_two[...].reshape(FULL, FULL)
    for out in outs:
        out.wait()


def first_stage(first_a, first_b, middle_a, middle_b):
    square = jax.ShapeDtypeStruct((FULL, FULL), jnp.float32)
    vmem = pl.BlockSpec(memory_space=pltpu.VMEM)
    whole = pl.BlockSpec(memory_space=pl.ANY)
    tall = RANK * MODES
    return pl.pallas_call(
        gram_kernel,
        out_shape=(square,) * 3,
        in_specs=[whole] * 4,
        out_specs=(vmem, whole, whole),
        scratch_shapes=[
            pltpu.VMEM((2, MODES, RANK), jnp.float32),
            pltpu.VMEM((2, tall, RANK), jnp.float32),
            pltpu.VMEM((PIECES, 8, FULL), jnp.float32),
            pltpu.VMEM((PIECES, 8, FULL), jnp.float32),
            pltpu.VMEM((PIECES, 8, FULL), jnp.float32),
            pltpu.VMEM((PIECES, 8, FULL), jnp.float32),
            pltpu.VMEM((2, CHIPS, 8, FULL), jnp.float32),
            pltpu.VMEM((2, PIECES, 8, FULL), jnp.float32),
            pltpu.VMEM((2, CHIPS - 1, 8, FULL), jnp.float32),
            pltpu.VMEM((2, 8, FULL), jnp.float32),
            pltpu.VMEM((2, DEPTH - 1, 8, FULL), jnp.float32),
            pltpu.VMEM((2, MODES, RANK, FULL), jnp.bfloat16),
            pltpu.VMEM((2, FULL, tall), jnp.bfloat16),
            pltpu.VMEM((2, tall, FULL), jnp.bfloat16),
            pltpu.VMEM((tall, FULL), jnp.bfloat16),
            pltpu.VMEM((FULL, FULL), jnp.float32),
            pltpu.VMEM((FULL, FULL), jnp.float32),
            pltpu.VMEM((FULL, FULL), jnp.float32),
            pltpu.SemaphoreType.DMA((2,)),
            pltpu.SemaphoreType.DMA((4,)),
            pltpu.SemaphoreType.DMA((2, 5)),
            pltpu.SemaphoreType.DMA((2, 5)),
        ],
        compiler_params=pltpu.CompilerParams(
            collective_id=0, has_side_effects=True, vmem_limit_bytes=VMEM_BYTES
        ),
    )(first_a, first_b, middle_a.reshape(tall, RANK), middle_b.reshape(tall, RANK))


def finish_kernel(
    gram_two, factor_one, inverse_one, first_a, first_b, middle_a, middle_b, last_a, last_b,
    ortho_first, ortho_middle, next_core,
    squares, zeros, first, held, carried, following, last_pairs, top_parts, low_pairs, load_sem, store_sem,
):
    loads = []
    places = [squares.at[0], squares.at[1], first.at[0], first.at[1]] + [held.at[index] for index in range(4)]
    sources = (factor_one, inverse_one, first_a, first_b, middle_a, middle_b, last_a, last_b)
    for index, (source, target) in enumerate(zip(sources, places)):
        load = pltpu.make_async_copy(source, target, load_sem.at[index])
        load.start()
        loads.append(load)
    tall = RANK * MODES

    def pair_of(source, mode):
        return jnp.concatenate(split(held[source, pl.ds(mode, RANK, stride=MODES), :]), axis=1)

    def twice(pair):
        return jnp.concatenate([pair, pair], axis=0)

    def factor_pairs(factor):
        corner = jnp.concatenate(split(factor[:RANK, :RANK]), axis=1)
        column = jnp.concatenate(split(factor[:, RANK:]), axis=1)
        return corner, column

    def carry(pairs, block_a, block_b, target, mode):
        by_a = dot_half(pairs[0], twice(block_a))
        by_b = dot_half(pairs[1], twice(block_b))
        by_a = by_a[:, :RANK] + by_a[:, RANK:]
        by_b = by_b[:, :RANK] + by_b[:, RANK:]
        if target is carried:
            target[0, pl.ds(mode, RANK, stride=MODES)] = by_a
            target[1, pl.ds(mode, FULL, stride=MODES)] = by_b
        else:
            target[0, pl.ds(mode * RANK, RANK)] = by_a
            target[1, pl.ds(mode * FULL, FULL)] = by_b
            start_store(target.at[0, pl.ds(mode * RANK, RANK)], next_core.at[pl.ds(0, RANK), mode, pl.ds(0, RANK)])
            start_store(target.at[1, pl.ds(mode * FULL, FULL)], next_core.at[:, mode, pl.ds(RANK, RANK)])

    stores = []

    def start_store(source, target):
        store = pltpu.make_async_copy(source, target, store_sem.at[len(stores)])
        store.start()
        stores.append(store)

    def send(buffer, target, part):
        for side in (0, 1):
            store = pltpu.make_async_copy(
                buffer.at[side, part], target.at[part, pl.ds(side * RANK, RANK)], store_sem.at[len(stores)]
            )
            store.start()
            stores.append(store)

    pairs_one = []

    def begin():
        for load in loads[:6]:
            load.wait()
        pairs_one.extend(factor_pairs(squares[0]))
        first_rows = jnp.concatenate([first[0], first[1]], axis=1)
        ortho_first[...] = dot_f32(first_rows, squares[1], ((1,), (1,)))
        zero = jnp.zeros((tall, RANK), jnp.float32)
        carried[0, pl.ds(tall, tall)] = zero
        zeros[...] = jnp.zeros_like(zeros)
        start_store(zeros, next_core.at[pl.ds(RANK, RANK), :, pl.ds(0, RANK)])
        start_store(carried.at[0, pl.ds(tall, tall)], ortho_middle.at[pl.ds(tall, tall), pl.ds(0, RANK)])

    def carry_middle(mode):
        carry(pairs_one, pair_of(0, mode), pair_of(1, mode), carried, mode)

    def prepare_last(mode):
        if mode == 0:
            loads[6].wait()
            loads[7].wait()
        last_pairs[0, mode] = pair_of(2, mode)
        last_pairs[1, mode] = pair_of(3, mode)

    chunk = 512

    def prepare_rows(start):
        part = pl.ds(start, chunk)
        high, low = split(jnp.concatenate([carried[0, part], carried[1, part]], axis=1))
        top_parts[0, part] = high
        top_parts[1, part] = low
        low_pairs[part] = jnp.concatenate(split(carried[1, pl.ds(tall + start, chunk)]), axis=1)

    tasks = [begin]
    tasks += [lambda mode=mode: carry_middle(mode) for mode in range(MODES)]
    tasks += [lambda start=start: prepare_rows(start) for start in range(0, tall, chunk)]
    tasks += [lambda mode=mode: (prepare_last(mode), prepare_last(mode + 1)) for mode in range(0, MODES, 2)]
    steps = factor_steps(gram_two[...], (64, 64, 64, 64), 16)
    for index in range(FULL // 16):
        next(steps)
        for task in tasks[2 * index - 2 : 2 * index] if index else []:
            task()
    factor_two, inverse_two = next(steps)

    pairs_two = factor_pairs(factor_two)
    for mode in range(MODES):
        carry(pairs_two, last_pairs[0, mode], last_pairs[1, mode], following, mode)
    inverse = inverse_two.T
    high, low = split(inverse)
    corner = twice(jnp.concatenate([high[RANK:, RANK:], low[RANK:, RANK:]], axis=1))
    for start in range(0, tall, chunk):
        part = pl.ds(start, chunk)
        result = dot_half(top_parts[0, part], high) + (
            dot_half(top_parts[1, part], high) + dot_half(top_parts[0, part], low)
        )
        carried[0, part] = result[:, :RANK]
        carried[1, part] = result[:, RANK:]
        send(carried, ortho_middle, part)
    for start in range(0, tall, chunk):
        result = dot_half(low_pairs[pl.ds(start, chunk)], corner)
        part = pl.ds(tall + start, chunk)
        carried[1, part] = result[:, :RANK] + result[:, RANK:]
        start_store(carried.at[1, part], ortho_middle.at[part, pl.ds(RANK, RANK)])
    for store in stores:
        store.wait()


def finish(gram_two, factor_one, inverse_one, first_a, first_b, *blocks):
    vmem = pl.BlockSpec(memory_space=pltpu.VMEM)
    whole = pl.BlockSpec(memory_space=pl.ANY)
    rows, tall = FULL * MODES, RANK * MODES
    flat = [block.reshape(tall, RANK) for block in blocks]
    ortho_first, ortho_middle, next_core = pl.pallas_call(
        finish_kernel,
        out_shape=(
            jax.ShapeDtypeStruct((MODES, FULL), jnp.float32),
            jax.ShapeDtypeStruct((rows, FULL), jnp.float32),
            jax.ShapeDtypeStruct((FULL, MODES, FULL), jnp.float32),
        ),
        in_specs=[vmem] + [whole] * 8,
        out_specs=(vmem, whole, whole),
        scratch_shapes=[
            pltpu.VMEM((2, FULL, FULL), jnp.float32),
            pltpu.VMEM((RANK, MODES, RANK), jnp.float32),
            pltpu.VMEM((2, MODES, RANK), jnp.float32),
            pltpu.VMEM((4, tall, RANK), jnp.float32),
            pltpu.VMEM((2, rows, RANK), jnp.float32),
            pltpu.VMEM((2, rows, RANK), jnp.float32),
            pltpu.VMEM((2, MODES, RANK, FULL), jnp.bfloat16),
            pltpu.VMEM((2, tall, FULL), jnp.bfloat16),
            pltpu.VMEM((tall, FULL), jnp.bfloat16),
            pltpu.SemaphoreType.DMA((8,)),
            pltpu.SemaphoreType.DMA((64,)),
        ],
        compiler_params=pltpu.CompilerParams(vmem_limit_bytes=VMEM_BYTES),
    )(gram_two, factor_one, inverse_one, first_a, first_b, *flat)
    shape = (FULL, MODES, FULL)
    return ortho_first, ortho_middle.reshape(shape), next_core.reshape(shape)


def body(first_a, first_b, middle_a, middle_b, last_a, last_b):
    gram_two, factor_one, inverse_one = first_stage(first_a, first_b, middle_a, middle_b)
    return finish(gram_two, factor_one, inverse_one, first_a, first_b, middle_a, middle_b, last_a, last_b)


def solution(mesh):
    placed = (
        P(("wide", "narrow"), None),
        P(("wide", "narrow"), None),
        P(None, ("wide", "narrow"), None),
        P(None, ("wide", "narrow"), None),
        P(None, ("wide", "narrow"), None),
        P(None, ("wide", "narrow"), None),
    )
    return jax.shard_map(
        body,
        mesh=mesh,
        in_specs=placed,
        out_specs=(
            P(("wide", "narrow"), None),
            P(None, ("wide", "narrow"), None),
            P(None, ("wide", "narrow"), None),
        ),
        check_vma=False,
    )
```

```python
import jax
import jax.numpy as jnp
from jax import lax
from jax.experimental import pallas as pl
from jax.experimental.pallas import tpu as pltpu
from jax.sharding import PartitionSpec as P

MESH = pl.DeviceIdType.MESH
HIGHEST_PRECISION = lax.Precision.HIGHEST
PIECES = 32
CHIPS = 16
SIDE = 4
DEPTH = 8
RANK = 128
FULL = 256
MODES = 16
VMEM_BYTES = 60 * 1024 * 1024


def dot_f32(left, right, dims):
    return lax.dot_general(
        left, right, (dims, ((), ())), precision=HIGHEST_PRECISION, preferred_element_type=jnp.float32
    )


def far_first(offsets, sizes):
    def hops(offset):
        return sum(min(step, size - step) for step, size in zip(offset, sizes))

    return sorted((offset for offset in offsets if any(offset)), key=lambda offset: -hops(offset))


PLANE_STEPS = far_first([(x, y) for x in range(SIDE) for y in range(SIDE)], (SIDE, SIDE))
LINE_STEPS = far_first([(z,) for z in range(DEPTH)], (DEPTH,))


def split(value):
    high = value.astype(jnp.bfloat16)
    return high, (value - high.astype(jnp.float32)).astype(jnp.bfloat16)


def dot_half(left, right):
    return jnp.dot(left, right, preferred_element_type=jnp.float32)


def factor_steps(square, widths, block, refs=None):
    rest = square
    start = 0
    uppers, lowers = [], []
    for panel_rows in widths:
        stop = start + panel_rows
        if refs is not None and start:
            rest = refs[2][pl.ds(start, FULL - start), :]
        halves = [rest[:panel_rows, :128], rest[:panel_rows, 128:]]
        below = rest[panel_rows:]
        done = []
        for base in range(start, stop, block):
            side, lane = base // 128, base % 128
            height = stop - base
            lanes = lax.broadcasted_iota(jnp.int32, (height, 128), 1)
            rows = lax.broadcasted_iota(jnp.int32, (height, 128), 0)
            columns = [
                jnp.broadcast_to(halves[side][:, lane + t : lane + t + 1], (height, 128)) for t in range(block)
            ]
            inside = (lanes >= lane) & (lanes < lane + block)
            halves[side] = jnp.where(inside, jnp.where(lanes == rows + lane, 1.0, 0.0), halves[side])
            for t in range(block):
                inverse = 1.0 / columns[t][t : t + 1]
                column = jnp.where(rows > t, columns[t], 0.0)
                factors = column * inverse
                for later in range(t + 1, block):
                    entry = columns[later][t : t + 1]
                    taken = (column * entry) * inverse if later == t + 1 else factors * entry
                    columns[later] = columns[later] - taken
                halves = [half - factors * half[t : t + 1] for half in halves]
            small, small_lanes = rows[:block], lanes[:block]
            pivots, top = columns[0][:block], halves[side][:block]
            for t in range(block):
                pivots = jnp.where(small == t, columns[t][:block], pivots)
                top = jnp.where(small_lanes == lane + t, columns[t][:block], top)
            root = lax.rsqrt(pivots)
            ready = [half[:block] * root for half in halves]
            done.append(jnp.concatenate(ready, axis=1))
            top = top * root
            upper = [top, ready[1]] if side == 0 else [ready[0], top]
            row = small + base
            uppers.append(
                jnp.concatenate([jnp.where(small_lanes + 128 * s >= row, upper[s], 0.0) for s in (0, 1)], axis=1)
            )
            lowers.append(
                jnp.concatenate([jnp.where(small_lanes + 128 * s <= row, ready[s], 0.0) for s in (0, 1)], axis=1)
            )
            halves = [half[block:] for half in halves]
            if base + block == stop and stop < FULL:
                done = jnp.concatenate(done, axis=0)
                row_index = lax.broadcasted_iota(jnp.int32, (panel_rows, FULL), 0) + start
                lane_index = lax.broadcasted_iota(jnp.int32, (panel_rows, FULL), 1)
                right = jnp.where((lane_index > row_index) & (lane_index < stop), 0.0, done)
                low = stop // 128 * 128
                update = dot_f32(done[:, low:], right, ((0,), (0,)))[stop - low :]
                below_lanes = lax.broadcasted_iota(jnp.int32, below.shape, 1)
                rest = jnp.where((below_lanes >= start) & (below_lanes < stop), 0.0, below) - update
                if refs is not None:
                    refs[2][pl.ds(stop, FULL - stop), :] = rest
            if refs is not None:
                refs[0][pl.ds(base, block), :] = uppers.pop()
                refs[1][pl.ds(base, block), :] = lowers.pop()
            yield
        start = stop
    yield jnp.concatenate(uppers, axis=0), jnp.concatenate(lowers, axis=0)


def gram_kernel(
    first_a, first_b, middle_a, middle_b, gram_two, factor_one, inverse_one,
    first_rows, held, local_one, local_two, total_one, total_two,
    half_in, half_out, part_in, piece_out, piece_in, pairs, pairs_turned, carried_top, carried_low, rest, factor_held, inverse_held,
    out_sem, load_sem, send_sem, recv_sem,
):
    wide = lax.axis_index("wide")
    core = lax.axis_index("narrow")
    spot_x = wide // 32
    spot_z = (wide // 4) % 8
    spot_y = wide % 4
    mine = core * CHIPS + spot_x * SIDE + spot_y
    base = core * CHIPS
    other = (wide, 1 - core)

    def plane_peer(step):
        x, y = (spot_x + step[0]) % SIDE, (spot_y + step[1]) % SIDE
        return base + x * SIDE + y, (x * 32 + spot_z * 4 + y, core)

    def line_device(step):
        return (spot_x * 32 + ((spot_z + step[0]) % DEPTH) * 4 + spot_y, core)

    loads = []
    for index, (source, target) in enumerate(
        ((first_a, first_rows.at[0]), (first_b, first_rows.at[1]), (middle_a, held.at[0]), (middle_b, held.at[1]))
    ):
        load = pltpu.make_async_copy(source, target, load_sem.at[index])
        load.start()
        loads.append(load)

    barrier = pltpu.get_barrier_semaphore()
    for step in LINE_STEPS:
        pl.semaphore_signal(barrier, inc=1, device_id=line_device(step), device_id_type=MESH)
    for step in PLANE_STEPS:
        pl.semaphore_signal(barrier, inc=1, device_id=plane_peer(step)[1], device_id_type=MESH)
    pl.semaphore_signal(barrier, inc=1, device_id=other, device_id_type=MESH)

    loads[0].wait()
    loads[1].wait()
    rows = jnp.concatenate([first_rows[0], first_rows[1]], axis=1)
    local_one[...] = dot_f32(rows, rows, ((0,), (0,))).reshape(PIECES, 8, FULL)
    pl.semaphore_wait(barrier, len(LINE_STEPS) + len(PLANE_STEPS) + 1)

    sent = []

    def reduce_all(turn, local, total, scale, meanwhile):
        def start(phase, source, target, device):
            pltpu.make_async_remote_copy(
                src_ref=source,
                dst_ref=target,
                send_sem=send_sem.at[turn, phase],
                recv_sem=recv_sem.at[turn, phase],
                device_id=device,
                device_id_type=MESH,
            ).start()

        def finish_phase(phase, buffer):
            copy = pltpu.make_async_remote_copy(
                src_ref=buffer,
                dst_ref=buffer,
                send_sem=send_sem.at[turn, phase],
                recv_sem=recv_sem.at[turn, phase],
                device_id=other,
                device_id_type=MESH,
            )
            copy.wait_recv()
            sent.append(copy)

        own_half = pl.ds(base, CHIPS)
        start(0, local.at[pl.ds(CHIPS - base, CHIPS)], half_in.at[turn], other)
        finish_phase(0, half_in.at[turn])
        half_out[turn, own_half] = local[own_half] + half_in[turn]

        for index, step in enumerate(PLANE_STEPS):
            peer, device = plane_peer(step)
            start(1, half_out.at[turn, peer], part_in.at[turn, index], device)
        meanwhile(1)
        finish_phase(1, part_in.at[turn])
        piece_out[turn] = half_out[turn, mine] + jnp.sum(part_in[turn], axis=0)

        for index, step in enumerate(LINE_STEPS):
            start(2, piece_out.at[turn], piece_in.at[turn, index], line_device(step))
        meanwhile(2)
        finish_phase(2, piece_in.at[turn])
        total[mine] = (piece_out[turn] + jnp.sum(piece_in[turn], axis=0)) * scale

        for step in PLANE_STEPS:
            start(3, total.at[mine], total.at[mine], plane_peer(step)[1])
        meanwhile(3)
        finish_phase(3, total.at[pl.ds(0, CHIPS - 1)])
        start(4, total.at[own_half], total.at[own_half], other)
        meanwhile(4)
        finish_phase(4, total.at[own_half])

    def prepare(phase):
        if phase > 1:
            return
        for side in (0, 1):
            loads[2 + side].wait()
            for mode in range(MODES):
                pair = jnp.concatenate(split(held[side, pl.ds(mode, RANK, stride=MODES), :]), axis=1)
                pairs[side, mode] = pair
                pairs_turned[side, :, mode * RANK : (mode + 1) * RANK] = pair.T

    reduce_all(0, local_one, total_one, 1.0 / 4096, prepare)
    gram = total_one[...].reshape(FULL, FULL)
    corner = jnp.concatenate(split(gram[:RANK, :RANK]), axis=1)
    column = jnp.concatenate(split(gram[:, RANK:]), axis=1)
    for mode in range(MODES):
        place = pl.ds(mode * RANK, RANK)
        pair_a, pair_b = pairs[0, mode], pairs[1, mode]
        by_a = dot_half(corner, jnp.concatenate([pair_a, pair_a], axis=0))
        by_b = dot_half(column, jnp.concatenate([pair_b, pair_b], axis=0))
        by_a = by_a[:, :RANK] + by_a[:, RANK:]
        by_b = by_b[:, :RANK] + by_b[:, RANK:]
        high, low = split(jnp.concatenate([by_a, by_b[:RANK]], axis=1))
        carried_top[0, place] = high
        carried_top[1, place] = low
        carried_low[place] = jnp.concatenate(split(by_b[RANK:]), axis=1)
    turned_a, turned_b = pairs_turned[0], pairs_turned[1]
    top = dot_half(turned_a, carried_top[0])
    top = top[:RANK] + (top[RANK:] + dot_half(turned_a[:RANK], carried_top[1]))
    low = dot_half(turned_b, carried_low[...])
    low = low[:RANK, :RANK] + (low[RANK:, :RANK] + (low[:RANK, RANK:] + low[RANK:, RANK:]))
    local_two[pl.ds(0, CHIPS)] = top.reshape(CHIPS, 8, FULL)
    local_two[pl.ds(CHIPS, CHIPS)] = jnp.concatenate([top[:, RANK:].T, low], axis=1).reshape(CHIPS, 8, FULL)
    steps = factor_steps(gram, (88, 88, 80), 8, (factor_held, inverse_held, rest))

    outs = [
        pltpu.make_async_copy(source, target, out_sem.at[index])
        for index, (source, target) in enumerate(((factor_held, factor_one), (inverse_held, inverse_one)))
    ]

    def factorize(phase):
        for _ in range((0, 11, 11, 10, 0)[phase]):
            next(steps)
        if phase == 4:
            for out in outs:
                out.start()

    reduce_all(1, local_two, total_two, 1.0 / 1048576, factorize)
    gram_two[...] = total_two[...].reshape(FULL, FULL)
    for out in outs:
        out.wait()
    for copy in sent:
        copy.wait_send()


def first_stage(first_a, first_b, middle_a, middle_b):
    square = jax.ShapeDtypeStruct((FULL, FULL), jnp.float32)
    vmem = pl.BlockSpec(memory_space=pltpu.VMEM)
    whole = pl.BlockSpec(memory_space=pl.ANY)
    tall = RANK * MODES
    return pl.pallas_call(
        gram_kernel,
        out_shape=(square,) * 3,
        in_specs=[whole] * 4,
        out_specs=(vmem, whole, whole),
        scratch_shapes=[
            pltpu.VMEM((2, MODES, RANK), jnp.float32),
            pltpu.VMEM((2, tall, RANK), jnp.float32),
            pltpu.VMEM((PIECES, 8, FULL), jnp.float32),
            pltpu.VMEM((PIECES, 8, FULL), jnp.float32),
            pltpu.VMEM((PIECES, 8, FULL), jnp.float32),
            pltpu.VMEM((PIECES, 8, FULL), jnp.float32),
            pltpu.VMEM((2, CHIPS, 8, FULL), jnp.float32),
            pltpu.VMEM((2, PIECES, 8, FULL), jnp.float32),
            pltpu.VMEM((2, CHIPS - 1, 8, FULL), jnp.float32),
            pltpu.VMEM((2, 8, FULL), jnp.float32),
            pltpu.VMEM((2, DEPTH - 1, 8, FULL), jnp.float32),
            pltpu.VMEM((2, MODES, RANK, FULL), jnp.bfloat16),
            pltpu.VMEM((2, FULL, tall), jnp.bfloat16),
            pltpu.VMEM((2, tall, FULL), jnp.bfloat16),
            pltpu.VMEM((tall, FULL), jnp.bfloat16),
            pltpu.VMEM((FULL, FULL), jnp.float32),
            pltpu.VMEM((FULL, FULL), jnp.float32),
            pltpu.VMEM((FULL, FULL), jnp.float32),
            pltpu.SemaphoreType.DMA((2,)),
            pltpu.SemaphoreType.DMA((4,)),
            pltpu.SemaphoreType.DMA((2, 5)),
            pltpu.SemaphoreType.DMA((2, 5)),
        ],
        compiler_params=pltpu.CompilerParams(
            collective_id=0, has_side_effects=True, vmem_limit_bytes=VMEM_BYTES
        ),
    )(first_a, first_b, middle_a.reshape(tall, RANK), middle_b.reshape(tall, RANK))


def finish_kernel(
    gram_two, factor_one, inverse_one, first_a, first_b, middle_a, middle_b, last_a, last_b,
    ortho_first, ortho_middle, next_core,
    squares, zeros, first, held, carried, following, last_pairs, top_parts, low_pairs, load_sem, store_sem,
):
    loads = []
    places = [squares.at[0], squares.at[1], first.at[0], first.at[1]] + [held.at[index] for index in range(4)]
    sources = (factor_one, inverse_one, first_a, first_b, middle_a, middle_b, last_a, last_b)
    for index, (source, target) in enumerate(zip(sources, places)):
        load = pltpu.make_async_copy(source, target, load_sem.at[index])
        load.start()
        loads.append(load)
    tall = RANK * MODES

    def pair_of(source, mode):
        return jnp.concatenate(split(held[source, pl.ds(mode, RANK, stride=MODES), :]), axis=1)

    def twice(pair):
        return jnp.concatenate([pair, pair], axis=0)

    def factor_pairs(factor):
        corner = jnp.concatenate(split(factor[:RANK, :RANK]), axis=1)
        column = jnp.concatenate(split(factor[:, RANK:]), axis=1)
        return corner, column

    def carry(pairs, block_a, block_b, target, mode):
        by_a = dot_half(pairs[0], twice(block_a))
        by_b = dot_half(pairs[1], twice(block_b))
        by_a = by_a[:, :RANK] + by_a[:, RANK:]
        by_b = by_b[:, :RANK] + by_b[:, RANK:]
        if target is carried:
            target[0, pl.ds(mode, RANK, stride=MODES)] = by_a
            target[1, pl.ds(mode, FULL, stride=MODES)] = by_b
        else:
            target[0, pl.ds(mode * RANK, RANK)] = by_a
            target[1, pl.ds(mode * FULL, FULL)] = by_b
            start_store(target.at[0, pl.ds(mode * RANK, RANK)], next_core.at[pl.ds(0, RANK), mode, pl.ds(0, RANK)])
            start_store(target.at[1, pl.ds(mode * FULL, FULL)], next_core.at[:, mode, pl.ds(RANK, RANK)])

    stores = []

    def start_store(source, target):
        store = pltpu.make_async_copy(source, target, store_sem.at[len(stores)])
        store.start()
        stores.append(store)

    def send(buffer, target, part):
        for side in (0, 1):
            store = pltpu.make_async_copy(
                buffer.at[side, part], target.at[part, pl.ds(side * RANK, RANK)], store_sem.at[len(stores)]
            )
            store.start()
            stores.append(store)

    pairs_one = []

    def begin():
        for load in loads[:6]:
            load.wait()
        pairs_one.extend(factor_pairs(squares[0]))
        first_rows = jnp.concatenate([first[0], first[1]], axis=1)
        ortho_first[...] = dot_f32(first_rows, squares[1], ((1,), (1,)))
        zero = jnp.zeros((tall, RANK), jnp.float32)
        carried[0, pl.ds(tall, tall)] = zero
        zeros[...] = jnp.zeros_like(zeros)
        start_store(zeros, next_core.at[pl.ds(RANK, RANK), :, pl.ds(0, RANK)])
        start_store(carried.at[0, pl.ds(tall, tall)], ortho_middle.at[pl.ds(tall, tall), pl.ds(0, RANK)])

    def carry_middle(mode):
        carry(pairs_one, pair_of(0, mode), pair_of(1, mode), carried, mode)

    def prepare_last(mode):
        if mode == 0:
            loads[6].wait()
            loads[7].wait()
        last_pairs[0, mode] = pair_of(2, mode)
        last_pairs[1, mode] = pair_of(3, mode)

    chunk = 512

    def prepare_rows(start):
        part = pl.ds(start, chunk)
        high, low = split(jnp.concatenate([carried[0, part], carried[1, part]], axis=1))
        top_parts[0, part] = high
        top_parts[1, part] = low
        low_pairs[part] = jnp.concatenate(split(carried[1, pl.ds(tall + start, chunk)]), axis=1)

    tasks = [begin]
    tasks += [lambda mode=mode: carry_middle(mode) for mode in range(MODES)]
    tasks += [lambda start=start: prepare_rows(start) for start in range(0, tall, chunk)]
    tasks += [lambda mode=mode: (prepare_last(mode), prepare_last(mode + 1)) for mode in range(0, MODES, 2)]
    steps = factor_steps(gram_two[...], (64, 64, 64, 64), 16)
    for index in range(FULL // 16):
        next(steps)
        for task in tasks[2 * index - 2 : 2 * index] if index else []:
            task()
    factor_two, inverse_two = next(steps)

    pairs_two = factor_pairs(factor_two)
    for mode in range(MODES):
        carry(pairs_two, last_pairs[0, mode], last_pairs[1, mode], following, mode)
    inverse = inverse_two.T
    high, low = split(inverse)
    corner = twice(jnp.concatenate([high[RANK:, RANK:], low[RANK:, RANK:]], axis=1))
    for start in range(0, tall, chunk):
        part = pl.ds(start, chunk)
        result = dot_half(top_parts[0, part], high) + (
            dot_half(top_parts[1, part], high) + dot_half(top_parts[0, part], low)
        )
        carried[0, part] = result[:, :RANK]
        carried[1, part] = result[:, RANK:]
        send(carried, ortho_middle, part)
    for start in range(0, tall, chunk):
        result = dot_half(low_pairs[pl.ds(start, chunk)], corner)
        part = pl.ds(tall + start, chunk)
        carried[1, part] = result[:, :RANK] + result[:, RANK:]
        start_store(carried.at[1, part], ortho_middle.at[part, pl.ds(RANK, RANK)])
    for store in stores:
        store.wait()


def finish(gram_two, factor_one, inverse_one, first_a, first_b, *blocks):
    vmem = pl.BlockSpec(memory_space=pltpu.VMEM)
    whole = pl.BlockSpec(memory_space=pl.ANY)
    rows, tall = FULL * MODES, RANK * MODES
    flat = [block.reshape(tall, RANK) for block in blocks]
    ortho_first, ortho_middle, next_core = pl.pallas_call(
        finish_kernel,
        out_shape=(
            jax.ShapeDtypeStruct((MODES, FULL), jnp.float32),
            jax.ShapeDtypeStruct((rows, FULL), jnp.float32),
            jax.ShapeDtypeStruct((FULL, MODES, FULL), jnp.float32),
        ),
        in_specs=[vmem] + [whole] * 8,
        out_specs=(vmem, whole, whole),
        scratch_shapes=[
            pltpu.VMEM((2, FULL, FULL), jnp.float32),
            pltpu.VMEM((RANK, MODES, RANK), jnp.float32),
            pltpu.VMEM((2, MODES, RANK), jnp.float32),
            pltpu.VMEM((4, tall, RANK), jnp.float32),
            pltpu.VMEM((2, rows, RANK), jnp.float32),
            pltpu.VMEM((2, rows, RANK), jnp.float32),
            pltpu.VMEM((2, MODES, RANK, FULL), jnp.bfloat16),
            pltpu.VMEM((2, tall, FULL), jnp.bfloat16),
            pltpu.VMEM((tall, FULL), jnp.bfloat16),
            pltpu.SemaphoreType.DMA((8,)),
            pltpu.SemaphoreType.DMA((64,)),
        ],
        compiler_params=pltpu.CompilerParams(vmem_limit_bytes=VMEM_BYTES),
    )(gram_two, factor_one, inverse_one, first_a, first_b, *flat)
    shape = (FULL, MODES, FULL)
    return ortho_first, ortho_middle.reshape(shape), next_core.reshape(shape)


def body(first_a, first_b, middle_a, middle_b, last_a, last_b):
    gram_two, factor_one, inverse_one = first_stage(first_a, first_b, middle_a, middle_b)
    return finish(gram_two, factor_one, inverse_one, first_a, first_b, middle_a, middle_b, last_a, last_b)


def solution(mesh):
    placed = (
        P(("wide", "narrow"), None),
        P(("wide", "narrow"), None),
        P(None, ("wide", "narrow"), None),
        P(None, ("wide", "narrow"), None),
        P(None, ("wide", "narrow"), None),
        P(None, ("wide", "narrow"), None),
    )
    return jax.shard_map(
        body,
        mesh=mesh,
        in_specs=placed,
        out_specs=(
            P(("wide", "narrow"), None),
            P(None, ("wide", "narrow"), None),
            P(None, ("wide", "narrow"), None),
        ),
        check_vma=False,
    )
```
